32 devices in a mesh: groups: 2 (over y), tile: 4 (over z), vec: 4 (over x, core).
Axes of the slice: x: 2, y: 2, z: 4, core: 2. Of those that a mesh axis runs over, the one named last changes fastest.
Arguments:
- vectors: float32 [2, 256, 3, 8192], P(None, 'vec', None, ('groups', 'tile')), parts along dimension 3, may hold values from -6 to 6
- links: float32 [3, 2, 3, 3, 8192], P(None, None, None, None, ('groups', 'tile')), parts along dimension 4, may hold values from -2.5 to 2.5
- momenta: int32 [8, 3], replicated, may hold values from -2 to 2
- directions: int32 [2], replicated, may hold values from 0 to 5
Outputs:
- elementals: float32 [512, 2, 2, 8, 256], P(('groups', 'tile'), None, None, None, 'vec'), parts along dimension 0
The draws below stay inside these ranges and needn't reach their ends.
There are 2 independent parts, one for each index of `groups`. The reference program is written for one: setup_inputs(seed, part) draws one part's arguments, and reference() takes and returns one part's arrays. A program takes and returns all parts, laid end to end along the dimension named above; an argument that names none is the same for every part. Nothing has to cross between parts.
Inputs may be any that keep to these rules, and one draw needn't show every extreme that they name: directions 0, 1, 2 step forward along the first, second, third dimension; 3, 4, 5 step backward along them.
All inputs are finite; a program needn't handle non-finite values.
Results may differ from the reference program's by a relative error of at most 0.00012.
Values sent between devices are 32-bit elements; how exact they have to be, the bound alone decides.
No kernel may reach another device: no remote copies, remote signals or barrier semaphores. Data moves between devices by JAX's collectives and lax.ppermute only.
A program may use at most 128 MiB of HBM per device.

```python
import math
import jax
import jax.numpy as jnp
from jax import lax

NV = 256
LY = 16
LZ = 32
ITERS = 4
NMOM = 8
NDISP = 2
LX = 8
NSITES = 4096


def set_ends(entries, stream_key, least, top_value):
    longest = entries.shape.index(max(entries.shape))
    spots = []
    for shift in (0, 1):
        where = [jax.random.randint(jax.random.fold_in(stream_key, axis), (), 0, length) for axis, length in enumerate(entries.shape)]
        where[longest] = (where[longest] + shift) % entries.shape[longest]
        spots.append(tuple(where))
    return entries.at[spots[0]].set(least).at[spots[1]].set(top_value)


def block_scale(key, shape, pieces, smallest, top_value):
    gain = 1.0
    for position, shards_of in pieces:
        steps = jax.random.uniform(jax.random.fold_in(jax.random.fold_in(key, 6), position), (shards_of,), jnp.float32, smallest / len(pieces), top_value / len(pieces))
        gain = gain * jnp.repeat(jnp.exp(steps), shape[position] // shards_of).reshape((-1,) + (1,) * (len(shape) - 1 - position))
    return gain


def noise(stream_key, shape, width, limit, split=(), kind=jnp.bfloat16):
    values = jax.random.normal(stream_key, shape, jnp.float32) * width
    if len(split) > 0:
        values = block_scale(stream_key, shape, split, -0.22, 0.18) * values
    return jnp.clip(values, min=-limit, max=limit).astype(kind)


def setup_inputs(seed: int = 0, part: int = 0) -> dict:
    seeds = jax.random.split(jax.random.key(seed), 5)
    part_keys = jax.random.split(jax.random.fold_in(seeds[4], part), 5)
    return {
        "vectors": noise(part_keys[0], (2, NV, 3, NSITES), 1.0, 6.0, ((1, 4), (3, 4)), jnp.float32),
        "links": noise(part_keys[1], (3, 2, 3, 3, NSITES), 6 ** -0.5, 2.5, ((4, 4),), jnp.float32),
        "momenta": set_ends(jax.random.randint(seeds[2], (NMOM, 3), -2, 3), jax.random.fold_in(seeds[2], 1), -2, 2).astype(jnp.int32),
        "directions": jax.random.randint(seeds[3], (NDISP,), 0, 6).astype(jnp.int32),
    }


hop_scale = 0.125

def link_apply(link_real, link_imag, field_real, field_imag, dagger):
    if dagger:
        link_real = jnp.swapaxes(link_real, 0, 1)
        link_imag = -jnp.swapaxes(link_imag, 0, 1)
    out_real = 0.0
    out_imag = 0.0
    for column in range(3):
        left_real = link_real[:, column][None]
        left_imag = link_imag[:, column][None]
        right_real = field_real[:, column][:, None]
        right_imag = field_imag[:, column][:, None]
        out_real = out_real + left_real * right_real - left_imag * right_imag
        out_imag = out_imag + left_real * right_imag + left_imag * right_real
    return (out_real, out_imag)

def hop_field(source, forward, backward):
    total_real = 0.0
    total_imag = 0.0
    for spatial in range(3):
        ahead = jnp.roll(source, -1, axis=3 + spatial)
        behind = jnp.roll(source, 1, axis=3 + spatial)
        ahead_real, ahead_imag = link_apply(forward[spatial][0], forward[spatial][1], ahead[0], ahead[1], False)
        behind_real, behind_imag = link_apply(backward[spatial][0], backward[spatial][1], behind[0], behind[1], True)
        total_real = total_real + ahead_real + behind_real
        total_imag = total_imag + ahead_imag + behind_imag
    return hop_scale * jnp.stack([total_real, total_imag])

def phases(momenta, flat_index, extent_x):
    plane_size = LY * LZ
    coord_x = flat_index // plane_size
    coord_y = flat_index % plane_size // LZ
    coord_z = flat_index % LZ
    part_x = jnp.mod(momenta[:, 0:1] * coord_x[None], extent_x).astype(jnp.float32) / extent_x
    part_y = jnp.mod(momenta[:, 1:2] * coord_y[None], LY).astype(jnp.float32) / LY
    part_z = jnp.mod(momenta[:, 2:3] * coord_z[None], LZ).astype(jnp.float32) / LZ
    angle = 2.0 * math.pi * (part_x + part_y + part_z)
    return (jnp.cos(angle), jnp.sin(angle))

def right_matrix(right_stack):
    disp_count = right_stack.shape[0]
    column_count = right_stack.shape[2]
    flat_real = right_stack[:, 0].reshape(disp_count, column_count, -1)
    flat_imag = right_stack[:, 1].reshape(disp_count, column_count, -1)
    real_side = jnp.concatenate([flat_real, flat_imag], axis=2)
    imag_side = jnp.concatenate([flat_imag, -flat_real], axis=2)
    return jnp.stack([real_side, imag_side], axis=1)

def twist_left(left_field, cos_row, sin_row):
    row_count = left_field.shape[1]
    twisted_real = cos_row * left_field[0] - sin_row * left_field[1]
    twisted_imag = cos_row * left_field[1] + sin_row * left_field[0]
    return jnp.concatenate([twisted_real.reshape(row_count, -1), twisted_imag.reshape(row_count, -1)], axis=1)

def elemental_each(left_field, right_mat, cosine, sine, norm_factor):

    def one_momentum(phase_pair):
        left_flat = twist_left(left_field, phase_pair[0], phase_pair[1])
        return jnp.einsum('ik,dcjk->idcj', left_flat, right_mat, precision=lax.Precision.HIGHEST)
    result = lax.map(one_momentum, (cosine, sine))
    return jnp.transpose(result, (1, 2, 3, 0, 4)) * norm_factor

def reference(vectors, links, momenta, directions):
    field = vectors.reshape(2, NV, 3, LX, LY, LZ)
    gauge = links.reshape(3, 2, 3, 3, LX, LY, LZ)
    forward = [gauge[spatial] for spatial in range(3)]
    backward = [jnp.roll(gauge[spatial], 1, axis=3 + spatial) for spatial in range(3)]
    previous = field
    current = hop_field(field, forward, backward)
    for order in range(ITERS - 1):
        following = 2.0 * hop_field(current, forward, backward) - previous
        previous, current = (current, following)
    filtered = current

    def make_branch(heading):
        spatial = heading % 3
        if heading < 3:

            def branch_fn():
                ahead = jnp.roll(filtered, -1, axis=3 + spatial)
                return jnp.stack(link_apply(forward[spatial][0], forward[spatial][1], ahead[0], ahead[1], False))
        else:

            def branch_fn():
                behind = jnp.roll(filtered, 1, axis=3 + spatial)
                return jnp.stack(link_apply(backward[spatial][0], backward[spatial][1], behind[0], behind[1], True))
        return branch_fn
    branches = [make_branch(heading) for heading in range(6)]
    displaced = [lax.switch(directions[disp_slot], branches) for disp_slot in range(NDISP)]
    right_stack = jnp.stack(displaced).reshape(NDISP, 2, NV, 3, NSITES)
    flat_index = jnp.arange(NSITES, dtype=jnp.int32)
    cosine, sine = phases(momenta, flat_index, LX)
    norm_factor = 1.0 / math.sqrt(3.0 * NSITES)
    right_mat = right_matrix(right_stack)
    return elemental_each(filtered.reshape(2, NV, 3, NSITES), right_mat, cosine, sine, norm_factor)
```

```python
import functools
import math

import jax
import jax.numpy as jnp
from jax import lax
from jax.experimental import pallas as pl
from jax.experimental.pallas import tpu as pltpu
from jax.sharding import PartitionSpec as P

LY = 16
LZ = 32
ITERS = 4
LANES = 128
PLANE = LY * LZ
QP = PLANE // LANES
YLO = LANES // LZ

hop_scale = 0.125


def piece_coords(mode, tile, tiles, k, lane):
    wy = (LY // tiles) * LZ
    bz = LZ // tiles
    if mode == 0:
        site = k * LANES + lane
        return site // PLANE, site % PLANE // LZ, site % LZ
    if mode == 1:
        flat = k * LANES + lane
        return flat // wy, tile * (LY // tiles) + flat % wy // LZ, lane % LZ
    slot = k * tiles + (lane % LZ) // bz
    return slot // QP, YLO * (slot % QP) + lane // LZ, tile * bz + lane % bz


def piece_index(mode, tile, tiles, x, y, z):
    wy = (LY // tiles) * LZ
    bz = LZ // tiles
    if mode == 0:
        site = x * PLANE + y * LZ + z
        return site // LANES, site % LANES
    if mode == 1:
        flat = x * wy + (y - tile * (LY // tiles)) * LZ + z
        return flat // LANES, flat % LANES
    slot = x * QP + y // YLO
    return slot // tiles, (y % YLO) * LZ + (slot % tiles) * bz + (z - tile * bz)


def pack_piece(mode, tiles, tile, read, write, kt):
    lane = lax.broadcasted_iota(jnp.int32, (1, LANES), 1)
    if mode == 0:
        for k in range(kt):
            write(k, read(tile * kt + k))
    elif mode == 1:
        wy = (LY // tiles) * LZ
        if wy >= LANES:
            per = wy // LANES
            for k in range(kt):
                write(k, read((k // per) * QP + tile * per + k % per))
        else:
            nx = LANES // wy
            row = (tile * wy) // LANES
            off = (tile * wy) % LANES
            for k in range(kt):
                out = None
                for j in range(nx):
                    part = pltpu.roll(read((k * nx + j) * QP + row), lax.rem(w_shift(wy * j - off), LANES), 1)
                    out = part if out is None else jnp.where(lane // wy == j, part, out)
                write(k, out)
    else:
        bz = LZ // tiles
        for k in range(kt):
            out = None
            for slot in range(tiles):
                index = k * tiles + slot
                part = pltpu.roll(read(index), lax.rem(w_shift((slot - tile) * bz), LANES), 1)
                out = part if out is None else jnp.where((lane % LZ) // bz == slot, part, out)
            write(k, out)


def w_shift(shift):
    return shift + 2 * LANES


def filter_kernel(tiles, kt, scal, field_ref, link_ref, piece_ref, glink_ref, a_ref, b_ref, l_ref):
    comps = 6
    nt = tiles * kt
    lx = nt // QP
    lane = lax.broadcasted_iota(jnp.int32, (1, LANES), 1)
    depth = lane % LZ
    rows = field_ref.shape[2]

    def at(x, q):
        return x * QP + q

    def moved(get, n, axis, step):
        x, q = n // QP, lax.rem(n, QP)
        if axis == 0:
            return get(at(lax.rem(x + step + lx, lx), q))
        if axis == 1:
            here, there = get(n), get(at(x, lax.rem(q + step + QP, QP)))
            if step > 0:
                return rolled(jnp.where(lane < LZ, there, here), LANES - LZ)
            return rolled(jnp.where(lane >= LANES - LZ, there, here), LZ)
        here = get(n)
        if step > 0:
            return jnp.where(depth == LZ - 1, rolled(here, LZ - 1), rolled(here, LANES - 1))
        return jnp.where(depth == 0, rolled(here, LANES - LZ + 1), rolled(here, 1))

    def rolled(value, shift):
        return pltpu.roll(value, shift, value.ndim - 1)

    def load_slab(t, carry):
        for k in range(kt):
            for c in range(comps):
                a_ref[t * kt + k, c] = field_ref[t, c, :, k * LANES : (k + 1) * LANES]
            for m in range(3):
                l_ref[m, t * kt + k] = link_ref[t, m, :, k * LANES : (k + 1) * LANES]
        return carry

    lax.fori_loop(0, tiles, load_slab, 0)

    def shift_links(n, carry):
        for m in range(3):
            l_ref[3 + m, n] = moved(lambda i: l_ref[m, i], n, m, -1)
        return carry

    lax.fori_loop(0, nt, shift_links, 0)

    def hop(src, n):
        acc = [None] * comps
        for m in range(3):
            for side in (0, 1):
                near = [moved(lambda i: src[i, c], n, m, 1 - 2 * side) for c in range(comps)]
                for i in range(3):
                    for j in range(3):
                        row = i * 3 + j if side == 0 else j * 3 + i
                        lr = l_ref[3 * side + m, n, row : row + 1, :]
                        li = l_ref[3 * side + m, n, 9 + row : 10 + row, :]
                        fr, fi = near[j], near[3 + j]
                        if side == 0:
                            re = lr * fr - li * fi
                            im = lr * fi + li * fr
                        else:
                            re = lr * fr + li * fi
                            im = lr * fi - li * fr
                        acc[i] = re if acc[i] is None else acc[i] + re
                        acc[3 + i] = im if acc[3 + i] is None else acc[3 + i] + im
        return acc

    src, dst = a_ref, b_ref
    for order in range(ITERS):

        def body(n, carry, src=src, dst=dst, order=order):
            acc = hop(src, n)
            for c in range(comps):
                if order == 0:
                    dst[n, c] = hop_scale * acc[c]
                else:
                    dst[n, c] = (2.0 * hop_scale) * acc[c] - dst[n, c]
            return carry

        lax.fori_loop(0, nt, body, 0)
        src, dst = dst, src

    slots = glink_ref.shape[0]
    mine = scal[1]
    for mode in range(3):

        @pl.when(scal[0] == mode)
        def _():
            def one_piece(t, carry):
                for c in range(comps):

                    def write(k, value, c=c):
                        piece_ref[t, k, c] = value

                    pack_piece(mode, tiles, t, lambda n, c=c: src[n, c], write, kt)
                return carry

            lax.fori_loop(0, tiles, one_piece, 0)
            for slot in range(slots):

                def write(k, value, slot=slot):
                    glink_ref[slot, k] = value

                pack_piece(mode, tiles, mine, lambda n, slot=slot: l_ref[scal[2 + slot], n], write, kt)


def contract_kernel(
    nvt, slots, moms, norm, scal, left_ref, own_ref, trig_ref, glink_ref, index_ref, out_ref, whi, wlo, dhi, dlo, acc_ref
):
    k = pl.program_id(0)
    vecs, tiles = left_ref.shape[0], left_ref.shape[1]
    rows = vecs * tiles * nvt
    cols = tiles * nvt
    comps = 6
    kt = pl.num_programs(0)

    def split(value):
        high = value.astype(jnp.bfloat16)
        return high, (value - high.astype(jnp.float32)).astype(jnp.bfloat16)

    for v in range(vecs):
        for t in range(tiles):
            base = (v * tiles + t) * nvt
            for c in range(3):
                rh, rl = split(left_ref[v, t, 0, c])
                ih, il = split(left_ref[v, t, 0, 3 + c])
                for ref, re, im in ((whi, rh, ih), (wlo, rl, il)):
                    ref[base : base + nvt, c * LANES : (c + 1) * LANES] = re
                    ref[base : base + nvt, (3 + c) * LANES : (4 + c) * LANES] = im
                    ref[rows + base : rows + base + nvt, c * LANES : (c + 1) * LANES] = -im
                    ref[rows + base : rows + base + nvt, (3 + c) * LANES : (4 + c) * LANES] = re

    for slot in range(slots):
        ka, kb = scal[slot, k], scal[slot, kt + k]
        forward = scal[slot, 2 * kt] > 0
        sign = jnp.where(forward, 1.0, -1.0)
        lanes = jnp.broadcast_to(index_ref[slot, k, 0:1, :], (nvt, LANES))
        take_b = jnp.broadcast_to(index_ref[slot, k, 1:2, :], (nvt, LANES)) > 0
        link = []
        for i in range(3):
            for j in range(3):
                row = jnp.where(forward, i * 3 + j, j * 3 + i)
                link.append((glink_ref[slot, k, pl.ds(row, 1), :], sign * glink_ref[slot, k, pl.ds(9 + row, 1), :]))
        for t in range(tiles):
            near = []
            for c in range(comps):
                first = jnp.take_along_axis(own_ref[t, ka, c], lanes, axis=1)
                second = jnp.take_along_axis(own_ref[t, kb, c], lanes, axis=1)
                near.append(jnp.where(take_b, second, first))
            for i in range(3):
                dr, di = 0.0, 0.0
                for j in range(3):
                    lr, li = link[i * 3 + j]
                    dr = dr + lr * near[j] - li * near[3 + j]
                    di = di + lr * near[3 + j] + li * near[j]
                for p in range(moms):
                    co = trig_ref[k, p : p + 1, :]
                    si = trig_ref[k, moms + p : moms + p + 1, :]
                    base = ((slot * moms + p) * tiles + t) * nvt
                    for half, value in ((0, co * dr + si * di), (1, co * di - si * dr)):
                        high, low = split(value)
                        at = (half * 3 + i) * LANES
                        dhi[base : base + nvt, at : at + LANES] = high
                        dlo[base : base + nvt, at : at + LANES] = low

    step = 256

    @pl.when(k == 0)
    def _():
        acc_ref[...] = jnp.zeros_like(acc_ref)

    def mul(m, carry):
        at = pl.ds(pl.multiple_of(m * step, step), step)
        dims = (((1,), (1,)), ((), ()))
        dot = functools.partial(lax.dot_general, dimension_numbers=dims, preferred_element_type=jnp.float32)
        acc_ref[at, :] += dot(dhi[at, :], whi[...]) + (dot(dhi[at, :], wlo[...]) + dot(dlo[at, :], whi[...]))
        return carry

    lax.fori_loop(0, acc_ref.shape[0] // step, mul, 0)

    @pl.when(k == kt - 1)
    def _():
        per = moms * cols
        for slot in range(slots):
            for part in range(2):
                block = acc_ref[slot * per : (slot + 1) * per, part * rows : (part + 1) * rows]
                at = (slot * 2 + part) * per
                out_ref[:, at : at + per] = norm * block.T


def local(vectors, links, momenta, directions):
    nv = vectors.shape[1]
    sites = vectors.shape[3]
    tiles = lax.axis_size("tile")
    vecs = lax.axis_size("vec")
    tile = lax.axis_index("tile")
    slots = directions.shape[0]
    moms = momenta.shape[0]
    nvt = nv // tiles
    kt = sites // LANES
    nt = kt * tiles
    extent_x = sites * tiles // PLANE
    norm = 1.0 / math.sqrt(3.0 * sites * tiles)
    f32 = jnp.float32

    gauge = lax.all_gather(links.reshape(3, 18, sites), "tile", axis=0)
    field = jnp.transpose(vectors, (0, 2, 1, 3)).reshape(6, tiles, nvt, sites)
    field = lax.all_to_all(jnp.transpose(field, (1, 0, 2, 3)), "tile", 0, 0)

    heading = directions % 3
    uses_y = jnp.any(heading == 1)
    uses_x = jnp.any(heading == 0)
    mode = jnp.where(uses_y, jnp.where(uses_x, 2, 0), 1).astype(jnp.int32)

    scal = jnp.concatenate([jnp.stack([mode, tile.astype(jnp.int32)]), directions.astype(jnp.int32)])
    smem = pl.BlockSpec(memory_space=pltpu.SMEM)
    vmem = pl.BlockSpec(memory_space=pltpu.VMEM)
    piece, glink = pl.pallas_call(
        functools.partial(filter_kernel, tiles, kt),
        out_shape=(
            jax.ShapeDtypeStruct((tiles, kt, 6, nvt, LANES), f32),
            jax.ShapeDtypeStruct((slots, kt, 18, LANES), f32),
        ),
        in_specs=[smem, vmem, vmem],
        out_specs=(vmem, vmem),
        scratch_shapes=[
            pltpu.VMEM((nt, 6, nvt, LANES), f32),
            pltpu.VMEM((nt, 6, nvt, LANES), f32),
            pltpu.VMEM((6, nt, 18, LANES), f32),
        ],
        compiler_params=pltpu.CompilerParams(vmem_limit_bytes=48 << 20),
        name="chebyshev",
    )(scal, field, gauge)

    own = lax.all_to_all(piece, "tile", 0, 0)
    left = lax.all_gather(own, "vec", axis=0)

    k = jnp.arange(kt, dtype=jnp.int32)[:, None]
    lane = jnp.arange(LANES, dtype=jnp.int32)[None]

    def pick(options):
        return jnp.where(mode == 0, options[0], jnp.where(mode == 1, options[1], options[2]))

    coords = [piece_coords(m, tile, tiles, k, lane) for m in range(3)]
    x, y, z = (pick([jnp.broadcast_to(c[axis], (kt, LANES)) for c in coords]) for axis in range(3))
    start_x = jnp.where(mode == 0, tile * (sites // PLANE), 0)

    def part(axis, coord, extent):
        return jnp.mod(momenta[:, axis, None, None] * coord[None], extent).astype(f32) / extent

    angle = 2.0 * math.pi * (part(0, x + start_x, extent_x) + part(1, y, LY) + part(2, z, LZ))
    trig = jnp.transpose(jnp.concatenate([jnp.cos(angle), jnp.sin(angle)]), (1, 0, 2))

    index, spots = [], []
    for slot in range(slots):
        d = directions[slot]
        step = jnp.where(d < 3, 1, -1)
        xs = jnp.mod(x + jnp.where(heading[slot] == 0, step, 0), extent_x)
        ys = jnp.mod(y + jnp.where(heading[slot] == 1, step, 0), LY)
        zs = jnp.mod(z + jnp.where(heading[slot] == 2, step, 0), LZ)
        found = [piece_index(m, tile, tiles, xs, ys, zs) for m in range(3)]
        ks, ls = (pick([f[i] for f in found]) for i in range(2))
        ka, kb = jnp.min(ks, axis=1), jnp.max(ks, axis=1)
        index.append(jnp.stack([ls, (ks == kb[:, None]).astype(jnp.int32)], axis=1))
        spots.append(jnp.concatenate([ka, kb, (d < 3).astype(jnp.int32)[None]]))
    index, spots = jnp.stack(index), jnp.stack(spots).astype(jnp.int32)

    rows, cols = nv * vecs, nv
    bf16 = jnp.bfloat16
    partial_rows = pl.pallas_call(
        functools.partial(contract_kernel, nvt, slots, moms, norm),
        grid=(kt,),
        out_shape=jax.ShapeDtypeStruct((rows, slots * 2 * moms * cols), f32),
        in_specs=[
            smem,
            pl.BlockSpec((vecs, tiles, 1, 6, nvt, LANES), lambda i: (0, 0, i, 0, 0, 0)),
            vmem,
            vmem,
            vmem,
            vmem,
        ],
        out_specs=vmem,
        scratch_shapes=[
            pltpu.VMEM((2 * rows, 6 * LANES), bf16),
            pltpu.VMEM((2 * rows, 6 * LANES), bf16),
            pltpu.VMEM((slots * moms * cols, 6 * LANES), bf16),
            pltpu.VMEM((slots * moms * cols, 6 * LANES), bf16),
            pltpu.VMEM((slots * moms * cols, 2 * rows), f32),
        ],
        compiler_params=pltpu.CompilerParams(vmem_limit_bytes=48 << 20),
        name="contract",
    )(spots, left, own, trig, glink, index)
    mine = lax.psum_scatter(partial_rows, "tile", scatter_dimension=0, tiled=True)
    return mine.reshape(nv * vecs // tiles, slots, 2, moms, cols)


def solution(mesh):
    return jax.shard_map(
        local,
        mesh=mesh,
        in_specs=(
            P(None, "vec", None, ("groups", "tile")),
            P(None, None, None, None, ("groups", "tile")),
            P(),
            P(),
        ),
        out_specs=P(("groups", "tile"), None, None, None, "vec"),
        check_vma=False,
    )
```

```python
import functools
import math

import jax
import jax.numpy as jnp
from jax import lax
from jax.experimental import pallas as pl
from jax.experimental.pallas import tpu as pltpu
from jax.sharding import PartitionSpec as P

LY = 16
LZ = 32
ITERS = 4
LANES = 128
PLANE = LY * LZ
QP = PLANE // LANES
YLO = LANES // LZ

hop_scale = 0.125


def piece_coords(mode, tile, tiles, k, lane):
    wy = (LY // tiles) * LZ
    bz = LZ // tiles
    if mode == 0:
        site = k * LANES + lane
        return site // PLANE, site % PLANE // LZ, site % LZ
    if mode == 1:
        flat = k * LANES + lane
        return flat // wy, tile * (LY // tiles) + flat % wy // LZ, lane % LZ
    slot = k * tiles + (lane % LZ) // bz
    return slot // QP, YLO * (slot % QP) + lane // LZ, tile * bz + lane % bz


def piece_index(mode, tile, tiles, x, y, z):
    wy = (LY // tiles) * LZ
    bz = LZ // tiles
    if mode == 0:
        site = x * PLANE + y * LZ + z
        return site // LANES, site % LANES
    if mode == 1:
        flat = x * wy + (y - tile * (LY // tiles)) * LZ + z
        return flat // LANES, flat % LANES
    slot = x * QP + y // YLO
    return slot // tiles, (y % YLO) * LZ + (slot % tiles) * bz + (z - tile * bz)


def pack_piece(mode, tiles, tile, read, write, kt):
    lane = lax.broadcasted_iota(jnp.int32, (1, LANES), 1)
    wy = (LY // tiles) * LZ
    bz = LZ // tiles

    def joined(indices, shifts, owner):
        out = None
        for j, (index, shift) in enumerate(zip(indices, shifts)):
            part = pltpu.roll(read(index), lax.rem(shift + 2 * LANES, LANES), 1)
            out = part if out is None else jnp.where(owner == j, part, out)
        return out

    def one(k, carry):
        if mode == 0:
            value = read(tile * kt + k)
        elif mode == 1 and wy >= LANES:
            per = wy // LANES
            value = read((k // per) * QP + tile * per + k % per)
        elif mode == 1:
            nx = LANES // wy
            first = k * nx * QP + (tile * wy) // LANES
            off = (tile * wy) % LANES
            value = joined([first + j * QP for j in range(nx)], [wy * j - off for j in range(nx)], lane // wy)
        else:
            shifts = [(j - tile) * bz for j in range(tiles)]
            value = joined([k * tiles + j for j in range(tiles)], shifts, (lane % LZ) // bz)
        write(k, value)
        return carry

    lax.fori_loop(0, kt, one, 0, unroll=tiles <= 4)


def filter_kernel(tiles, kt, rows, with_links, *refs):
    scal, slab_refs, refs = refs[0], refs[1 : 1 + tiles], refs[1 + tiles :]
    if with_links:
        piece_refs, (glink_ref, l_ref, a_ref, b_ref) = refs[:tiles], refs[tiles:]
    else:
        l_ref, piece_refs, (a_ref, b_ref) = refs[0], refs[1 : 1 + tiles], refs[1 + tiles :]
    mine = scal[1]
    comps = 6
    nt = tiles * kt
    lx = nt // QP
    lane = lax.broadcasted_iota(jnp.int32, (1, LANES), 1)
    depth = lane % LZ

    def at(x, q):
        return x * QP + q

    def moved(get, n, axis, step):
        x, q = n // QP, lax.rem(n, QP)
        if axis == 0:
            return get(at(lax.rem(x + step + lx, lx), q))
        if axis == 1:
            here, there = get(n), get(at(x, lax.rem(q + step + QP, QP)))
            if step > 0:
                return rolled(jnp.where(lane < LZ, there, here), LANES - LZ)
            return rolled(jnp.where(lane >= LANES - LZ, there, here), LZ)
        here = get(n)
        if step > 0:
            return jnp.where(depth == LZ - 1, rolled(here, LZ - 1), rolled(here, LANES - 1))
        return jnp.where(depth == 0, rolled(here, LANES - LZ + 1), rolled(here, 1))

    def rolled(value, shift):
        return pltpu.roll(value, shift, value.ndim - 1)

    for s in range(tiles):
        t = lax.rem(mine - s + tiles, tiles)
        for k in range(kt):
            lanes = slice(k * LANES, (k + 1) * LANES)
            for c in range(comps):
                a_ref[t * kt + k, c] = slab_refs[s][c * rows : (c + 1) * rows, lanes]
            if with_links:
                for m in range(3):
                    first = comps * rows + 18 * m
                    l_ref[m, t * kt + k] = slab_refs[s][first : first + 18, lanes]

    if with_links:

        def shift_links(n, carry):
            for m in range(3):
                l_ref[3 + m, n] = moved(lambda i: l_ref[m, i], n, m, -1)
            return carry

        lax.fori_loop(0, nt, shift_links, 0)

    def hop(src, n):
        acc = [None] * comps
        for m in range(3):
            for side in (0, 1):
                near = [moved(lambda i: src[i, c], n, m, 1 - 2 * side) for c in range(comps)]
                for i in range(3):
                    for j in range(3):
                        row = i * 3 + j if side == 0 else j * 3 + i
                        lr = l_ref[3 * side + m, n, row : row + 1, :]
                        li = l_ref[3 * side + m, n, 9 + row : 10 + row, :]
                        fr, fi = near[j], near[3 + j]
                        if side == 0:
                            re = lr * fr - li * fi
                            im = lr * fi + li * fr
                        else:
                            re = lr * fr + li * fi
                            im = lr * fi - li * fr
                        acc[i] = re if acc[i] is None else acc[i] + re
                        acc[3 + i] = im if acc[3 + i] is None else acc[3 + i] + im
        return acc

    src, dst = a_ref, b_ref
    for order in range(ITERS):

        def body(n, carry, src=src, dst=dst, order=order):
            acc = hop(src, n)
            for c in range(comps):
                if order == 0:
                    dst[n, c] = hop_scale * acc[c]
                else:
                    dst[n, c] = (2.0 * hop_scale) * acc[c] - dst[n, c]
            return carry

        lax.fori_loop(0, nt, body, 0)
        src, dst = dst, src

    for mode in range(3):

        @pl.when(scal[0] == mode)
        def _():
            for s in range(tiles):
                for c in range(comps):

                    def write(k, value, s=s, c=c):
                        piece_refs[s][k, c] = value

                    pack_piece(mode, tiles, lax.rem(mine + s, tiles), lambda n, c=c: src[n, c], write, kt)
            if with_links:
                for slot in range(glink_ref.shape[0]):

                    def write(k, value, slot=slot):
                        glink_ref[slot, k] = value

                    pack_piece(mode, tiles, mine, lambda n, slot=slot: l_ref[scal[2 + slot], n], write, kt)


def contract_kernel(chunks, slots, moms, norm, scal, left_ref, *refs):
    own_refs = refs[:chunks]
    trig_ref, glink_ref, index_ref, out_ref, side, disp, whole, dhi, dlo, acc_ref = refs[chunks:]
    k = pl.program_id(0)
    vecs, tiles, nvc = left_ref.shape[0], left_ref.shape[1], left_ref.shape[4]
    rows = vecs * tiles * nvc
    cols = tiles * nvc * chunks
    comps = 6
    kt = pl.num_programs(0)
    depth = comps * LANES
    group = dhi.shape[1]
    per = group // cols
    half = 3 * LANES

    mine = scal[slots, 0]

    def split(value):
        high = value.astype(jnp.bfloat16)
        return high, (value - high.astype(jnp.float32)).astype(jnp.bfloat16)

    def place(s, outer, count):
        if nvc % 8:
            return (outer * tiles + s) * count
        return pl.multiple_of((outer * tiles + lax.rem(mine - s + tiles, tiles)) * count, 8)

    @pl.when(k == 0)
    def _():
        acc_ref[...] = jnp.zeros_like(acc_ref)

    for v in range(vecs):
        for t in range(tiles):
            at = pl.ds(place(t, v, nvc), nvc)
            for c in range(comps):
                side[at, c * LANES : (c + 1) * LANES] = left_ref[v, t, 0, c]
    for c in range(3):
        rh, rl = split(side[:, c * LANES : (c + 1) * LANES])
        ih, il = split(side[:, half + c * LANES : half + (c + 1) * LANES])
        for third, re, im in ((0, rh, ih), (1, rl, il), (2, rh, ih)):
            first = third * depth + c * LANES
            whole[0:rows, first : first + LANES] = re
            whole[0:rows, first + half : first + half + LANES] = im
            whole[rows : 2 * rows, first : first + LANES] = -im
            whole[rows : 2 * rows, first + half : first + half + LANES] = re

    for slot in range(slots):
        ka, kb = scal[slot, k], scal[slot, kt + k]
        forward = scal[slot, 2 * kt] > 0
        sign = jnp.where(forward, 1.0, -1.0)
        lanes = jnp.broadcast_to(index_ref[slot, k, 0:1, :], (nvc, LANES))
        take_b = jnp.broadcast_to(index_ref[slot, k, 1:2, :], (nvc, LANES)) > 0
        link = []
        for i in range(3):
            for j in range(3):
                row = jnp.where(forward, i * 3 + j, j * 3 + i)
                link.append((glink_ref[slot, k, pl.ds(row, 1), :], sign * glink_ref[slot, k, pl.ds(9 + row, 1), :]))
        for t in range(tiles):
            for part in range(chunks):
                near = []
                for c in range(comps):
                    first = jnp.take_along_axis(own_refs[part][t, ka, c], lanes, axis=1)
                    second = jnp.take_along_axis(own_refs[part][t, kb, c], lanes, axis=1)
                    near.append(jnp.where(take_b, second, first))
                at = pl.ds(place(t, 0, chunks * nvc) + part * nvc, nvc)
                for i in range(3):
                    dr, di = 0.0, 0.0
                    for j in range(3):
                        lr, li = link[i * 3 + j]
                        dr = dr + lr * near[j] - li * near[3 + j]
                        di = di + lr * near[3 + j] + li * near[j]
                    disp[slot, i, at, :] = dr
                    disp[slot, 3 + i, at, :] = di

    for g in range(slots * moms // per):
        for r in range(per):
            slot, p = divmod(g * per + r, moms)
            co = trig_ref[k, p : p + 1, :]
            si = trig_ref[k, moms + p : moms + p + 1, :]
            for i in range(3):
                dr, di = disp[slot, i], disp[slot, 3 + i]
                for part, value in ((0, co * dr + si * di), (1, co * di - si * dr)):
                    high, low = split(value)
                    first = part * half + i * LANES
                    dhi[g, r * cols : (r + 1) * cols, first : first + LANES] = high
                    dlo[g, r * cols : (r + 1) * cols, first : first + LANES] = low
        high, low = dhi[g], dlo[g]
        acc_ref[g * group : (g + 1) * group, :] += lax.dot_general(
            jnp.concatenate([high, high, low], axis=1),
            whole[...],
            (((1,), (1,)), ((), ())),
            preferred_element_type=jnp.float32,
        )

    @pl.when(k == kt - 1)
    def _():
        span = moms * cols
        for slot in range(slots):
            for part in range(2):
                block = acc_ref[slot * span : (slot + 1) * span, part * rows : (part + 1) * rows]
                first = (slot * 2 + part) * span
                out_ref[:, first : first + span] = norm * block.T


def along_tiles(value, steps):
    if steps == 0:
        return value
    count = lax.axis_size("tile")
    return lax.ppermute(value, "tile", [(i, (i + steps) % count) for i in range(count)])


def local(vectors, links, momenta, directions):
    nv = vectors.shape[1]
    sites = vectors.shape[3]
    tiles = lax.axis_size("tile")
    vecs = lax.axis_size("vec")
    tile = lax.axis_index("tile")
    slots = directions.shape[0]
    moms = momenta.shape[0]
    nvt = nv // tiles
    chunks = 2 if nvt % 16 == 0 else 1
    nvc = nvt // chunks
    kt = sites // LANES
    nt = kt * tiles
    extent_x = sites * tiles // PLANE
    norm = 1.0 / math.sqrt(3.0 * sites * tiles)
    f32 = jnp.float32
    smem = pl.BlockSpec(memory_space=pltpu.SMEM)
    vmem = pl.BlockSpec(memory_space=pltpu.VMEM)

    heading = directions % 3
    uses_y = jnp.any(heading == 1)
    uses_x = jnp.any(heading == 0)
    mode = jnp.where(uses_y, jnp.where(uses_x, 2, 0), 1).astype(jnp.int32)
    scal = jnp.concatenate([jnp.stack([mode, tile.astype(jnp.int32)]), directions.astype(jnp.int32)])

    parts = jnp.transpose(vectors, (0, 2, 1, 3)).reshape(6, tiles, chunks, nvc, sites)
    parts = jnp.transpose(parts, (2, 1, 0, 3, 4)).reshape(chunks, tiles, 6 * nvc, sites)
    flat_links = links.reshape(54, sites)
    fields = []
    for c in range(chunks):
        sent = [lax.dynamic_index_in_dim(parts[c], lax.rem(tile + s, tiles), 0, keepdims=False) for s in range(tiles)]
        if c == 0:
            sent = [jnp.concatenate([block, flat_links]) for block in sent]
        else:
            fields[c - 1], sent = lax.optimization_barrier((fields[c - 1], sent))
        fields.append([along_tiles(block, s) for s, block in enumerate(sent)])

    piece_shapes = (jax.ShapeDtypeStruct((kt, 6, nvc, LANES), f32),) * tiles
    link_shape = (6, nt, 18, LANES)
    owns, lefts = [], []
    for c in range(chunks):
        scratch = [pltpu.VMEM((nt, 6, nvc, LANES), f32)] * 2
        call = functools.partial(
            pl.pallas_call,
            functools.partial(filter_kernel, tiles, kt, nvc, c == 0),
            scratch_shapes=scratch,
            compiler_params=pltpu.CompilerParams(vmem_limit_bytes=48 << 20),
            cost_estimate=pl.CostEstimate(
                flops=250 * ITERS * 432 * nvc * nt * LANES, bytes_accessed=48 * nvc * nt * LANES, transcendentals=0
            ),
            name="chebyshev",
        )
        if c == 0:
            *pieces, glink, turned = call(
                out_shape=(
                    *piece_shapes,
                    jax.ShapeDtypeStruct((slots, kt, 18, LANES), f32),
                    jax.ShapeDtypeStruct(link_shape, f32),
                ),
                in_specs=[smem] + [vmem] * tiles,
                out_specs=(vmem,) * (tiles + 2),
            )(scal, *fields[c])
        else:
            pieces = call(out_shape=piece_shapes, in_specs=[smem] + [vmem] * (tiles + 1), out_specs=(vmem,) * tiles)(
                scal, *fields[c], turned
            )
        if c + 1 < chunks:
            fields[c + 1], pieces = lax.optimization_barrier((fields[c + 1], pieces))
        if c > 0:
            own, pieces = lax.optimization_barrier((own, pieces))
            owns[c - 1] = jnp.stack(own)
        own = [along_tiles(pieces[s], s) for s in range(tiles)]
        owns.append(jnp.stack(own))
    for c in range(chunks):
        if nvc % 8:
            owns[c] = owns[c][jnp.mod(tile - jnp.arange(tiles, dtype=jnp.int32), tiles)]
        lefts.append(lax.all_gather(owns[c], "vec", axis=0))

    k = jnp.arange(kt, dtype=jnp.int32)[:, None]
    lane = jnp.arange(LANES, dtype=jnp.int32)[None]

    def pick(options):
        return jnp.where(mode == 0, options[0], jnp.where(mode == 1, options[1], options[2]))

    coords = [piece_coords(m, tile, tiles, k, lane) for m in range(3)]
    x, y, z = (pick([jnp.broadcast_to(c[axis], (kt, LANES)) for c in coords]) for axis in range(3))
    start_x = jnp.where(mode == 0, tile * (sites // PLANE), 0)

    def part(axis, coord, extent):
        return jnp.mod(momenta[:, axis, None, None] * coord[None], extent).astype(f32) / extent

    angle = 2.0 * math.pi * (part(0, x + start_x, extent_x) + part(1, y, LY) + part(2, z, LZ))
    trig = jnp.transpose(jnp.concatenate([jnp.cos(angle), jnp.sin(angle)]), (1, 0, 2))

    index, spots = [], []
    for slot in range(slots):
        d = directions[slot]
        step = jnp.where(d < 3, 1, -1)
        xs = jnp.mod(x + jnp.where(heading[slot] == 0, step, 0), extent_x)
        ys = jnp.mod(y + jnp.where(heading[slot] == 1, step, 0), LY)
        zs = jnp.mod(z + jnp.where(heading[slot] == 2, step, 0), LZ)
        found = [piece_index(m, tile, tiles, xs, ys, zs) for m in range(3)]
        ks, ls = (pick([f[i] for f in found]) for i in range(2))
        ka, kb = jnp.min(ks, axis=1), jnp.max(ks, axis=1)
        index.append(jnp.stack([ls, (ks == kb[:, None]).astype(jnp.int32)], axis=1))
        spots.append(jnp.concatenate([ka, kb, (d < 3).astype(jnp.int32)[None]]))
    spots.append(jnp.broadcast_to(tile.astype(jnp.int32), spots[0].shape))
    index, spots = jnp.stack(index), jnp.stack(spots).astype(jnp.int32)

    rows, cols = vecs * tiles * nvc, nv
    depth = 6 * LANES
    group = cols * max(1, min(moms, 256 // cols))
    groups = slots * moms * cols // group
    bf16 = jnp.bfloat16
    mine = []
    for c in range(chunks):
        partial_rows = pl.pallas_call(
            functools.partial(contract_kernel, chunks, slots, moms, norm),
            grid=(kt,),
            out_shape=jax.ShapeDtypeStruct((rows, slots * 2 * moms * cols), f32),
            in_specs=[smem, pl.BlockSpec((vecs, tiles, 1, 6, nvc, LANES), lambda i: (0, 0, i, 0, 0, 0))]
            + [vmem] * (chunks + 3),
            out_specs=vmem,
            scratch_shapes=[
                pltpu.VMEM((rows, depth), f32),
                pltpu.VMEM((slots, 6, cols, LANES), f32),
                pltpu.VMEM((2 * rows, 3 * depth), bf16),
                pltpu.VMEM((groups, group, depth), bf16),
                pltpu.VMEM((groups, group, depth), bf16),
                pltpu.VMEM((slots * moms * cols, 2 * rows), f32),
            ],
            compiler_params=pltpu.CompilerParams(vmem_limit_bytes=48 << 20),
            cost_estimate=pl.CostEstimate(
                flops=24 * rows * slots * moms * cols * 6 * sites, bytes_accessed=32 * rows * sites, transcendentals=0
            ),
            name="contract",
        )(spots, lefts[c], *owns, trig, glink, index)
        mine.append(lax.psum_scatter(partial_rows, "tile", scatter_dimension=0, tiled=True))
    mine = [m.reshape(-1, nvc, slots * 2 * moms * cols) for m in mine]
    return jnp.stack(mine, axis=1).reshape(nv * vecs // tiles, slots, 2, moms, cols)


def solution(mesh):
    return jax.shard_map(
        local,
        mesh=mesh,
        in_specs=(
            P(None, "vec", None, ("groups", "tile")),
            P(None, None, None, None, ("groups", "tile")),
            P(),
            P(),
        ),
        out_specs=P(("groups", "tile"), None, None, None, "vec"),
        check_vma=False,
    )
```

```python
import functools
import math

import jax
import jax.numpy as jnp
from jax import lax
from jax.experimental import pallas as pl
from jax.experimental.pallas import tpu as pltpu
from jax.sharding import PartitionSpec as P

LY = 16
LZ = 32
ITERS = 4
LANES = 128
PLANE = LY * LZ
QP = PLANE // LANES
YLO = LANES // LZ

hop_scale = 0.125


def piece_coords(mode, tile, tiles, k, lane):
    wy = (LY // tiles) * LZ
    bz = LZ // tiles
    if mode == 0:
        site = k * LANES + lane
        return site // PLANE, site % PLANE // LZ, site % LZ
    if mode == 1:
        flat = k * LANES + lane
        return flat // wy, tile * (LY // tiles) + flat % wy // LZ, lane % LZ
    slot = k * tiles + (lane % LZ) // bz
    return slot // QP, YLO * (slot % QP) + lane // LZ, tile * bz + lane % bz


def piece_index(mode, tile, tiles, x, y, z):
    wy = (LY // tiles) * LZ
    bz = LZ // tiles
    if mode == 0:
        site = x * PLANE + y * LZ + z
        return site // LANES, site % LANES
    if mode == 1:
        flat = x * wy + (y - tile * (LY // tiles)) * LZ + z
        return flat // LANES, flat % LANES
    slot = x * QP + y // YLO
    return slot // tiles, (y % YLO) * LZ + (slot % tiles) * bz + (z - tile * bz)


def pack_piece(mode, tiles, tile, read, write, kt):
    lane = lax.broadcasted_iota(jnp.int32, (1, LANES), 1)
    wy = (LY // tiles) * LZ
    bz = LZ // tiles

    def joined(indices, shifts, owner):
        out = None
        for j, (index, shift) in enumerate(zip(indices, shifts)):
            part = pltpu.roll(read(index), lax.rem(shift + 2 * LANES, LANES), 1)
            out = part if out is None else jnp.where(owner == j, part, out)
        return out

    def one(k, carry):
        if mode == 0:
            value = read(tile * kt + k)
        elif mode == 1 and wy >= LANES:
            per = wy // LANES
            value = read((k // per) * QP + tile * per + k % per)
        elif mode == 1:
            nx = LANES // wy
            first = k * nx * QP + (tile * wy) // LANES
            off = (tile * wy) % LANES
            value = joined([first + j * QP for j in range(nx)], [wy * j - off for j in range(nx)], lane // wy)
        else:
            shifts = [(j - tile) * bz for j in range(tiles)]
            value = joined([k * tiles + j for j in range(tiles)], shifts, (lane % LZ) // bz)
        write(k, value)
        return carry

    lax.fori_loop(0, kt, one, 0, unroll=tiles <= 4)


def filter_kernel(tiles, kt, rows, with_links, *refs):
    scal, slab_refs, refs = refs[0], refs[1 : 1 + tiles], refs[1 + tiles :]
    if with_links:
        link_ref, piece_refs, (glink_ref, l_ref, a_ref, b_ref) = refs[0], refs[1 : 1 + tiles], refs[1 + tiles :]
    else:
        l_ref, piece_refs, (a_ref, b_ref) = refs[0], refs[1 : 1 + tiles], refs[1 + tiles :]
    mine = scal[1]
    comps = 6
    nt = tiles * kt
    lx = nt // QP
    lane = lax.broadcasted_iota(jnp.int32, (1, LANES), 1)
    depth = lane % LZ

    def at(x, q):
        return x * QP + q

    def moved(get, n, axis, step):
        x, q = n // QP, lax.rem(n, QP)
        if axis == 0:
            return get(at(lax.rem(x + step + lx, lx), q))
        if axis == 1:
            here, there = get(n), get(at(x, lax.rem(q + step + QP, QP)))
            if step > 0:
                return rolled(jnp.where(lane < LZ, there, here), LANES - LZ)
            return rolled(jnp.where(lane >= LANES - LZ, there, here), LZ)
        here = get(n)
        if step > 0:
            return jnp.where(depth == LZ - 1, rolled(here, LZ - 1), rolled(here, LANES - 1))
        return jnp.where(depth == 0, rolled(here, LANES - LZ + 1), rolled(here, 1))

    def rolled(value, shift):
        return pltpu.roll(value, shift, value.ndim - 1)

    for s in range(tiles):
        t = lax.rem(mine - s + tiles, tiles)
        for k in range(kt):
            lanes = slice(k * LANES, (k + 1) * LANES)
            for c in range(comps):
                a_ref[t * kt + k, c] = slab_refs[s][c * rows : (c + 1) * rows, lanes]
            if with_links:
                share = link_ref.shape[3] // LANES
                lanes = slice(k % share * LANES, (k % share + 1) * LANES)
                for m in range(3):
                    l_ref[m, t * kt + k] = link_ref[k // share, s, 18 * m : 18 * m + 18, lanes]

    if with_links:

        def shift_links(n, carry):
            for m in range(3):
                l_ref[3 + m, n] = moved(lambda i: l_ref[m, i], n, m, -1)
            return carry

        lax.fori_loop(0, nt, shift_links, 0)

    def hop(src, n):
        acc = [None] * comps
        for m in range(3):
            for side in (0, 1):
                near = [moved(lambda i: src[i, c], n, m, 1 - 2 * side) for c in range(comps)]
                for i in range(3):
                    for j in range(3):
                        row = i * 3 + j if side == 0 else j * 3 + i
                        lr = l_ref[3 * side + m, n, row : row + 1, :]
                        li = l_ref[3 * side + m, n, 9 + row : 10 + row, :]
                        fr, fi = near[j], near[3 + j]
                        if side == 0:
                            re = lr * fr - li * fi
                            im = lr * fi + li * fr
                        else:
                            re = lr * fr + li * fi
                            im = lr * fi - li * fr
                        acc[i] = re if acc[i] is None else acc[i] + re
                        acc[3 + i] = im if acc[3 + i] is None else acc[3 + i] + im
        return acc

    src, dst = a_ref, b_ref
    for order in range(ITERS):

        def body(n, carry, src=src, dst=dst, order=order):
            acc = hop(src, n)
            for c in range(comps):
                if order == 0:
                    dst[n, c] = hop_scale * acc[c]
                else:
                    dst[n, c] = (2.0 * hop_scale) * acc[c] - dst[n, c]
            return carry

        lax.fori_loop(0, nt, body, 0)
        src, dst = dst, src

    for mode in range(3):

        @pl.when(scal[0] == mode)
        def _():
            for s in range(tiles):
                for c in range(comps):

                    def write(k, value, s=s, c=c):
                        piece_refs[s][k, c] = value

                    pack_piece(mode, tiles, lax.rem(mine + s, tiles), lambda n, c=c: src[n, c], write, kt)
            if with_links:
                for slot in range(glink_ref.shape[0]):

                    def write(k, value, slot=slot):
                        glink_ref[slot, k] = value

                    pack_piece(mode, tiles, mine, lambda n, slot=slot: l_ref[scal[2 + slot], n], write, kt)


def contract_kernel(vecs, chunks, slots, moms, norm, scal, *refs):
    left_refs, own_refs, refs = refs[:vecs], refs[vecs : vecs + chunks], refs[vecs + chunks :]
    tiles, nvc = own_refs[0].shape[0], own_refs[0].shape[3]
    (trig_ref, glink_ref, index_ref), out_refs, refs = refs[:3], refs[3 : 3 + tiles], refs[3 + tiles :]
    side, disp, whole, dhi, dlo, acc_ref, turned = refs
    k = pl.program_id(0)
    rows = vecs * tiles * nvc
    cols = tiles * nvc * chunks
    comps = 6
    kt = pl.num_programs(0)
    depth = comps * LANES
    group = dhi.shape[1]
    per = group // cols
    half = 3 * LANES

    mine = scal[slots, 0]

    def split(value):
        high = value.astype(jnp.bfloat16)
        return high, (value - high.astype(jnp.float32)).astype(jnp.bfloat16)

    def place(s, outer, count):
        if nvc % 8:
            return (outer * tiles + s) * count
        return pl.multiple_of((outer * tiles + lax.rem(mine - s + tiles, tiles)) * count, 8)

    @pl.when(k == 0)
    def _():
        acc_ref[...] = jnp.zeros_like(acc_ref)

    for v in range(vecs):
        for t in range(tiles):
            at = pl.ds(place(t, v if nvc % 8 else scal[slots + 1, v], nvc), nvc)
            for c in range(comps):
                side[at, c * LANES : (c + 1) * LANES] = left_refs[v][t, 0, c]
    for c in range(3):
        rh, rl = split(side[:, c * LANES : (c + 1) * LANES])
        ih, il = split(side[:, half + c * LANES : half + (c + 1) * LANES])
        for third, re, im in ((0, rh, ih), (1, rl, il), (2, rh, ih)):
            first = third * depth + c * LANES
            whole[0:rows, first : first + LANES] = re
            whole[0:rows, first + half : first + half + LANES] = im
            whole[rows : 2 * rows, first : first + LANES] = -im
            whole[rows : 2 * rows, first + half : first + half + LANES] = re

    for slot in range(slots):
        ka, kb = scal[slot, k], scal[slot, kt + k]
        forward = scal[slot, 2 * kt] > 0
        sign = jnp.where(forward, 1.0, -1.0)
        lanes = jnp.broadcast_to(index_ref[slot, k, 0:1, :], (nvc, LANES))
        take_b = jnp.broadcast_to(index_ref[slot, k, 1:2, :], (nvc, LANES)) > 0
        link = []
        for i in range(3):
            for j in range(3):
                row = jnp.where(forward, i * 3 + j, j * 3 + i)
                link.append((glink_ref[slot, k, pl.ds(row, 1), :], sign * glink_ref[slot, k, pl.ds(9 + row, 1), :]))
        for t in range(tiles):
            for part in range(chunks):
                near = []
                for c in range(comps):
                    first = jnp.take_along_axis(own_refs[part][t, ka, c], lanes, axis=1)
                    second = jnp.take_along_axis(own_refs[part][t, kb, c], lanes, axis=1)
                    near.append(jnp.where(take_b, second, first))
                at = pl.ds(place(t, 0, chunks * nvc) + part * nvc, nvc)
                for i in range(3):
                    dr, di = 0.0, 0.0
                    for j in range(3):
                        lr, li = link[i * 3 + j]
                        dr = dr + lr * near[j] - li * near[3 + j]
                        di = di + lr * near[3 + j] + li * near[j]
                    disp[slot, i, at, :] = dr
                    disp[slot, 3 + i, at, :] = di

    for g in range(slots * moms // per):
        for r in range(per):
            slot, p = divmod(g * per + r, moms)
            co = trig_ref[k, p : p + 1, :]
            si = trig_ref[k, moms + p : moms + p + 1, :]
            for i in range(3):
                dr, di = disp[slot, i], disp[slot, 3 + i]
                for part, value in ((0, co * dr + si * di), (1, co * di - si * dr)):
                    high, low = split(value)
                    first = part * half + i * LANES
                    dhi[g, r * cols : (r + 1) * cols, first : first + LANES] = high
                    dlo[g, r * cols : (r + 1) * cols, first : first + LANES] = low
        high, low = dhi[g], dlo[g]
        acc_ref[g * group : (g + 1) * group, :] += lax.dot_general(
            jnp.concatenate([high, high, low], axis=1),
            whole[...],
            (((1,), (1,)), ((), ())),
            preferred_element_type=jnp.float32,
        )

    @pl.when(k == kt - 1)
    def _():
        span = moms * cols
        for slot in range(slots):
            for part in range(2):
                block = acc_ref[slot * span : (slot + 1) * span, part * rows : (part + 1) * rows]
                first = (slot * 2 + part) * span
                turned[:, first : first + span] = norm * block.T
        part = rows // tiles
        for s in range(tiles):
            out_refs[s][...] = turned[pl.ds(pl.multiple_of(lax.rem(mine + s, tiles) * part, 8), part), :]


def along_tiles(value, steps):
    if steps == 0:
        return value
    count = lax.axis_size("tile")
    return lax.ppermute(value, "tile", [(i, (i + steps) % count) for i in range(count)])


def vec_cores():
    return 2 if lax.axis_size("vec") % 2 == 0 else 1


def over_chips(value):
    count = lax.axis_size("vec")
    blocks = [value]
    for step in range(vec_cores(), count, vec_cores()):
        blocks.append(lax.ppermute(value, "vec", [(i, (i + step) % count) for i in range(count)]))
    return blocks


def over_cores(blocks):
    if vec_cores() == 1:
        return []
    count = lax.axis_size("vec")
    return [lax.ppermute(block, "vec", [(i, i ^ 1) for i in range(count)]) for block in blocks]


def block_owners():
    count, here = lax.axis_size("vec"), lax.axis_index("vec")
    owner = [lax.rem(here - step + count, count) for step in range(0, count, vec_cores())]
    if vec_cores() == 2:
        owner += [other + 1 - 2 * (here % 2) for other in owner]
    return jnp.stack(owner).astype(jnp.int32)


def local(vectors, links, momenta, directions):
    nv = vectors.shape[1]
    sites = vectors.shape[3]
    tiles = lax.axis_size("tile")
    vecs = lax.axis_size("vec")
    tile = lax.axis_index("tile")
    slots = directions.shape[0]
    moms = momenta.shape[0]
    nvt = nv // tiles
    chunks = 2 if nvt % 16 == 0 else 1
    nvc = nvt // chunks
    kt = sites // LANES
    nt = kt * tiles
    extent_x = sites * tiles // PLANE
    norm = 1.0 / math.sqrt(3.0 * sites * tiles)
    f32 = jnp.float32
    smem = pl.BlockSpec(memory_space=pltpu.SMEM)
    vmem = pl.BlockSpec(memory_space=pltpu.VMEM)

    heading = directions % 3
    uses_y = jnp.any(heading == 1)
    uses_x = jnp.any(heading == 0)
    mode = jnp.where(uses_y, jnp.where(uses_x, 2, 0), 1).astype(jnp.int32)
    scal = jnp.concatenate([jnp.stack([mode, tile.astype(jnp.int32)]), directions.astype(jnp.int32)])

    parts = jnp.transpose(vectors, (0, 2, 1, 3)).reshape(6, tiles, chunks, nvc, sites)
    parts = jnp.transpose(parts, (2, 1, 0, 3, 4)).reshape(chunks, tiles, 6 * nvc, sites)
    share = sites // vecs
    link_share = lax.dynamic_slice_in_dim(links.reshape(54, sites), lax.axis_index("vec") * share, share, 1)
    gauge = lax.all_gather(jnp.stack([along_tiles(link_share, s) for s in range(tiles)]), "vec", axis=0)
    fields = []
    for c in range(chunks):
        sent = [lax.dynamic_index_in_dim(parts[c], lax.rem(tile + s, tiles), 0, keepdims=False) for s in range(tiles)]
        if c > 0:
            fields[c - 1], sent = lax.optimization_barrier((fields[c - 1], sent))
        fields.append([along_tiles(block, s) for s, block in enumerate(sent)])

    piece_shapes = (jax.ShapeDtypeStruct((kt, 6, nvc, LANES), f32),) * tiles
    link_shape = (6, nt, 18, LANES)
    owns, lefts = [], []
    for c in range(chunks):
        scratch = [pltpu.VMEM((nt, 6, nvc, LANES), f32)] * 2
        call = functools.partial(
            pl.pallas_call,
            functools.partial(filter_kernel, tiles, kt, nvc, c == 0),
            scratch_shapes=scratch,
            compiler_params=pltpu.CompilerParams(vmem_limit_bytes=48 << 20),
            cost_estimate=pl.CostEstimate(
                flops=250 * ITERS * 432 * nvc * nt * LANES, bytes_accessed=48 * nvc * nt * LANES, transcendentals=0
            ),
            name="chebyshev",
        )
        if c == 0:
            *pieces, glink, turned = call(
                out_shape=(
                    *piece_shapes,
                    jax.ShapeDtypeStruct((slots, kt, 18, LANES), f32),
                    jax.ShapeDtypeStruct(link_shape, f32),
                ),
                in_specs=[smem] + [vmem] * (tiles + 1),
                out_specs=(vmem,) * (tiles + 2),
            )(scal, *fields[c], gauge)
        else:
            pieces = call(out_shape=piece_shapes, in_specs=[smem] + [vmem] * (tiles + 1), out_specs=(vmem,) * tiles)(
                scal, *fields[c], turned
            )
        if c + 1 < chunks:
            fields[c + 1], pieces = lax.optimization_barrier((fields[c + 1], pieces))
        if c > 0:
            own, pieces = lax.optimization_barrier((own, pieces))
            owns[c - 1] = jnp.stack(own)
        own = [along_tiles(pieces[s], s) for s in range(tiles)]
        owns.append(jnp.stack(own))
    for c in range(chunks):
        if nvc % 8:
            owns[c] = owns[c][jnp.mod(tile - jnp.arange(tiles, dtype=jnp.int32), tiles)]
        lefts.append(over_chips(owns[c]))
        if c == 1:
            lefts[0][1:], owns[1] = lax.optimization_barrier((lefts[0][1:], owns[1]))
            lefts[1][0] = owns[1]
    owner = block_owners()

    k = jnp.arange(kt, dtype=jnp.int32)[:, None]
    lane = jnp.arange(LANES, dtype=jnp.int32)[None]

    def pick(options):
        return jnp.where(mode == 0, options[0], jnp.where(mode == 1, options[1], options[2]))

    coords = [piece_coords(m, tile, tiles, k, lane) for m in range(3)]
    x, y, z = (pick([jnp.broadcast_to(c[axis], (kt, LANES)) for c in coords]) for axis in range(3))
    start_x = jnp.where(mode == 0, tile * (sites // PLANE), 0)

    def part(axis, coord, extent):
        return jnp.mod(momenta[:, axis, None, None] * coord[None], extent).astype(f32) / extent

    angle = 2.0 * math.pi * (part(0, x + start_x, extent_x) + part(1, y, LY) + part(2, z, LZ))
    trig = jnp.transpose(jnp.concatenate([jnp.cos(angle), jnp.sin(angle)]), (1, 0, 2))

    index, spots = [], []
    for slot in range(slots):
        d = directions[slot]
        step = jnp.where(d < 3, 1, -1)
        xs = jnp.mod(x + jnp.where(heading[slot] == 0, step, 0), extent_x)
        ys = jnp.mod(y + jnp.where(heading[slot] == 1, step, 0), LY)
        zs = jnp.mod(z + jnp.where(heading[slot] == 2, step, 0), LZ)
        found = [piece_index(m, tile, tiles, xs, ys, zs) for m in range(3)]
        ks, ls = (pick([f[i] for f in found]) for i in range(2))
        ka, kb = jnp.min(ks, axis=1), jnp.max(ks, axis=1)
        index.append(jnp.stack([ls, (ks == kb[:, None]).astype(jnp.int32)], axis=1))
        spots.append(jnp.concatenate([ka, kb, (d < 3).astype(jnp.int32)[None]]))
    spots.append(jnp.broadcast_to(tile.astype(jnp.int32), spots[0].shape))
    spots.append(jnp.pad(owner, (0, 2 * kt + 1 - vecs)))
    index, spots = jnp.stack(index), jnp.stack(spots).astype(jnp.int32)

    rows, cols = vecs * tiles * nvc, nv
    depth = 6 * LANES
    group = cols * max(1, min(moms, 256 // cols))
    groups = slots * moms * cols // group
    bf16 = jnp.bfloat16
    mine = []
    for c in range(chunks):
        near, far = lefts[c][:1], lefts[c][1:]
        twins = over_cores(near)
        if c > 0:
            far, partial_rows = lax.optimization_barrier((far, partial_rows))
        left = near + far + twins + over_cores(far)
        if nvc % 8:
            left = list(jnp.stack(left)[jnp.argsort(owner)])
        if c > 0:
            mine.append(functools.reduce(jnp.add, [along_tiles(partial_rows[s], s) for s in range(tiles)]))
        partial_rows = pl.pallas_call(
            functools.partial(contract_kernel, vecs, chunks, slots, moms, norm),
            grid=(kt,),
            out_shape=(jax.ShapeDtypeStruct((rows // tiles, slots * 2 * moms * cols), f32),) * tiles,
            in_specs=[smem]
            + [pl.BlockSpec((tiles, 1, 6, nvc, LANES), lambda i: (0, i, 0, 0, 0))] * vecs
            + [vmem] * (chunks + 3),
            out_specs=(vmem,) * tiles,
            scratch_shapes=[
                pltpu.VMEM((rows, depth), f32),
                pltpu.VMEM((slots, 6, cols, LANES), f32),
                pltpu.VMEM((2 * rows, 3 * depth), bf16),
                pltpu.VMEM((groups, group, depth), bf16),
                pltpu.VMEM((groups, group, depth), bf16),
                pltpu.VMEM((slots * moms * cols, 2 * rows), f32),
                pltpu.VMEM((rows, slots * 2 * moms * cols), f32),
            ],
            compiler_params=pltpu.CompilerParams(vmem_limit_bytes=48 << 20),
            cost_estimate=pl.CostEstimate(
                flops=24 * rows * slots * moms * cols * 6 * sites, bytes_accessed=32 * rows * sites, transcendentals=0
            ),
            name="contract",
        )(spots, *left, *owns, trig, glink, index)
    mine.append(functools.reduce(jnp.add, [along_tiles(partial_rows[s], s) for s in range(tiles)]))
    mine = [m.reshape(-1, nvc, slots * 2 * moms * cols) for m in mine]
    return jnp.stack(mine, axis=1).reshape(nv * vecs // tiles, slots, 2, moms, cols)


def solution(mesh):
    return jax.shard_map(
        local,
        mesh=mesh,
        in_specs=(
            P(None, "vec", None, ("groups", "tile")),
            P(None, None, None, None, ("groups", "tile")),
            P(),
            P(),
        ),
        out_specs=P(("groups", "tile"), None, None, None, "vec"),
        check_vma=False,
    )
```

```python
import functools
import math

import jax
import jax.numpy as jnp
from jax import lax
from jax.experimental import pallas as pl
from jax.experimental.pallas import tpu as pltpu
from jax.sharding import PartitionSpec as P

LY = 16
LZ = 32
ITERS = 4
LANES = 128
PLANE = LY * LZ
QP = PLANE // LANES
YLO = LANES // LZ

hop_scale = 0.125


def piece_coords(mode, tile, tiles, k, lane):
    wy = (LY // tiles) * LZ
    bz = LZ // tiles
    if mode == 0:
        site = k * LANES + lane
        return site // PLANE, site % PLANE // LZ, site % LZ
    if mode == 1:
        flat = k * LANES + lane
        return flat // wy, tile * (LY // tiles) + flat % wy // LZ, lane % LZ
    slot = k * tiles + (lane % LZ) // bz
    return slot // QP, YLO * (slot % QP) + lane // LZ, tile * bz + lane % bz


def piece_index(mode, tile, tiles, x, y, z):
    wy = (LY // tiles) * LZ
    bz = LZ // tiles
    if mode == 0:
        site = x * PLANE + y * LZ + z
        return site // LANES, site % LANES
    if mode == 1:
        flat = x * wy + (y - tile * (LY // tiles)) * LZ + z
        return flat // LANES, flat % LANES
    slot = x * QP + y // YLO
    return slot // tiles, (y % YLO) * LZ + (slot % tiles) * bz + (z - tile * bz)


def pack_piece(mode, tiles, tile, read, write, kt):
    lane = lax.broadcasted_iota(jnp.int32, (1, LANES), 1)
    wy = (LY // tiles) * LZ
    bz = LZ // tiles

    def joined(indices, shifts, owner):
        out = None
        for j, (index, shift) in enumerate(zip(indices, shifts)):
            part = pltpu.roll(read(index), lax.rem(shift + 2 * LANES, LANES), 1)
            out = part if out is None else jnp.where(owner == j, part, out)
        return out

    def one(k, carry):
        if mode == 0:
            value = read(tile * kt + k)
        elif mode == 1 and wy >= LANES:
            per = wy // LANES
            value = read((k // per) * QP + tile * per + k % per)
        elif mode == 1:
            nx = LANES // wy
            first = k * nx * QP + (tile * wy) // LANES
            off = (tile * wy) % LANES
            value = joined([first + j * QP for j in range(nx)], [wy * j - off for j in range(nx)], lane // wy)
        else:
            shifts = [(j - tile) * bz for j in range(tiles)]
            value = joined([k * tiles + j for j in range(tiles)], shifts, (lane % LZ) // bz)
        write(k, value)
        return carry

    lax.fori_loop(0, kt, one, 0, unroll=tiles <= 4)


def filter_kernel(tiles, kt, rows, with_links, *refs):
    scal, slab_refs, refs = refs[0], refs[1 : 1 + tiles], refs[1 + tiles :]
    if with_links:
        link_ref, piece_refs, (glink_ref, l_ref, a_ref, b_ref) = refs[0], refs[1 : 1 + tiles], refs[1 + tiles :]
    else:
        l_ref, piece_refs, (a_ref, b_ref) = refs[0], refs[1 : 1 + tiles], refs[1 + tiles :]
    mine = scal[1]
    comps = 6
    nt = tiles * kt
    lx = nt // QP
    lane = lax.broadcasted_iota(jnp.int32, (1, LANES), 1)
    depth = lane % LZ

    def at(x, q):
        return x * QP + q

    def moved(get, x, q, axis, step):
        n = at(x, q)
        if axis == 0:
            return get(at(lax.rem(x + step + lx, lx), q))
        if axis == 1:
            here, there = get(n), get(at(x, (q + step) % QP))
            if step > 0:
                return rolled(jnp.where(lane < LZ, there, here), LANES - LZ)
            return rolled(jnp.where(lane >= LANES - LZ, there, here), LZ)
        here = get(n)
        if step > 0:
            return jnp.where(depth == LZ - 1, rolled(here, LZ - 1), rolled(here, LANES - 1))
        return jnp.where(depth == 0, rolled(here, LANES - LZ + 1), rolled(here, 1))

    def rolled(value, shift):
        return pltpu.roll(value, shift, value.ndim - 1)

    for s in range(tiles):
        t = lax.rem(mine - s + tiles, tiles)
        for k in range(kt):
            lanes = slice(k * LANES, (k + 1) * LANES)
            for c in range(comps):
                a_ref[t * kt + k, c] = slab_refs[s][c * rows : (c + 1) * rows, lanes]
            if with_links:
                share = link_ref.shape[3] // LANES
                lanes = slice(k % share * LANES, (k % share + 1) * LANES)
                for m in range(3):
                    l_ref[m, s * kt + k] = link_ref[k // share, s, 18 * m : 18 * m + 18, lanes]

    if with_links:

        def shift_links(x, carry):
            for q in range(QP):
                for m in range(3):
                    l_ref[3 + m, at(x, q)] = moved(lambda i: l_ref[m, i], x, q, m, -1)
            return carry

        lax.fori_loop(0, lx, shift_links, 0)

    def hop(src, x, q):
        n = at(x, q)
        acc = [None] * comps
        for m in range(3):
            for side in (0, 1):
                near = [moved(lambda i: src[i, c], x, q, m, 1 - 2 * side) for c in range(comps)]
                for i in range(3):
                    for j in range(3):
                        row = i * 3 + j if side == 0 else j * 3 + i
                        lr = l_ref[3 * side + m, n, row : row + 1, :]
                        li = l_ref[3 * side + m, n, 9 + row : 10 + row, :]
                        fr, fi = near[j], near[3 + j]
                        if side == 0:
                            re = lr * fr - li * fi
                            im = lr * fi + li * fr
                        else:
                            re = lr * fr + li * fi
                            im = lr * fi - li * fr
                        acc[i] = re if acc[i] is None else acc[i] + re
                        acc[3 + i] = im if acc[3 + i] is None else acc[3 + i] + im
        return acc

    src, dst = a_ref, b_ref
    for order in range(ITERS):

        def body(x, carry, src=src, dst=dst, order=order):
            for q in range(QP):
                n = x * QP + q
                acc = hop(src, x, q)
                for c in range(comps):
                    if order == 0:
                        dst[n, c] = hop_scale * acc[c]
                    else:
                        dst[n, c] = (2.0 * hop_scale) * acc[c] - dst[n, c]
            return carry

        lax.fori_loop(0, lx, body, 0)
        src, dst = dst, src

    for mode in range(3):

        @pl.when(scal[0] == mode)
        def _():
            for s in range(tiles):
                for c in range(comps):

                    def write(k, value, s=s, c=c):
                        piece_refs[s][k, c] = value

                    pack_piece(mode, tiles, lax.rem(mine + s, tiles), lambda n, c=c: src[n, c], write, kt)
            if with_links:
                for slot in range(glink_ref.shape[0]):

                    def write(k, value, slot=slot):
                        glink_ref[slot, k] = value

                    pack_piece(mode, tiles, mine, lambda n, slot=slot: l_ref[scal[2 + slot], n], write, kt)


def contract_kernel(vecs, chunks, slots, moms, norm, scal, *refs):
    left_refs, own_refs, refs = refs[:vecs], refs[vecs : vecs + chunks], refs[vecs + chunks :]
    tiles, nvc = own_refs[0].shape[0], own_refs[0].shape[3]
    (trig_ref, glink_ref, index_ref), out_refs, refs = refs[:3], refs[3 : 3 + tiles], refs[3 + tiles :]
    side, disp, whole, dhi, dlo, acc_ref, turned = refs
    k = pl.program_id(0)
    rows = vecs * tiles * nvc
    cols = tiles * nvc * chunks
    comps = 6
    kt = pl.num_programs(0)
    depth = comps * LANES
    group = dhi.shape[1]
    per = group // cols
    half = 3 * LANES

    mine = scal[slots, 0]

    def split(value):
        high = value.astype(jnp.bfloat16)
        return high, (value - high.astype(jnp.float32)).astype(jnp.bfloat16)

    def place(s, outer, count):
        if nvc % 8:
            return (outer * tiles + s) * count
        return pl.multiple_of((outer * tiles + lax.rem(mine - s + tiles, tiles)) * count, 8)

    @pl.when(k == 0)
    def _():
        acc_ref[...] = jnp.zeros_like(acc_ref)

    for v in range(vecs):
        for t in range(tiles):
            at = pl.ds(place(t, v if nvc % 8 else scal[slots + 1, v], nvc), nvc)
            for c in range(comps):
                side[at, c * LANES : (c + 1) * LANES] = left_refs[v][t, 0, c]
    for c in range(3):
        rh, rl = split(side[:, c * LANES : (c + 1) * LANES])
        ih, il = split(side[:, half + c * LANES : half + (c + 1) * LANES])
        for third, re, im in ((0, rh, ih), (1, rl, il), (2, rh, ih)):
            first = third * depth + c * LANES
            whole[0:rows, first : first + LANES] = re
            whole[0:rows, first + half : first + half + LANES] = im
            whole[rows : 2 * rows, first : first + LANES] = -im
            whole[rows : 2 * rows, first + half : first + half + LANES] = re

    for slot in range(slots):
        ka, kb = scal[slot, k], scal[slot, kt + k]
        forward = scal[slot, 2 * kt] > 0
        sign = jnp.where(forward, 1.0, -1.0)
        lanes = jnp.broadcast_to(index_ref[slot, k, 0:1, :], (nvc, LANES))
        take_b = jnp.broadcast_to(index_ref[slot, k, 1:2, :], (nvc, LANES)) > 0
        link = []
        for i in range(3):
            for j in range(3):
                row = jnp.where(forward, i * 3 + j, j * 3 + i)
                link.append((glink_ref[slot, k, pl.ds(row, 1), :], sign * glink_ref[slot, k, pl.ds(9 + row, 1), :]))
        for t in range(tiles):
            for part in range(chunks):
                near = []
                for c in range(comps):
                    first = jnp.take_along_axis(own_refs[part][t, ka, c], lanes, axis=1)
                    second = jnp.take_along_axis(own_refs[part][t, kb, c], lanes, axis=1)
                    near.append(jnp.where(take_b, second, first))
                at = pl.ds(place(t, 0, chunks * nvc) + part * nvc, nvc)
                for i in range(3):
                    dr, di = 0.0, 0.0
                    for j in range(3):
                        lr, li = link[i * 3 + j]
                        dr = dr + lr * near[j] - li * near[3 + j]
                        di = di + lr * near[3 + j] + li * near[j]
                    disp[slot, i, at, :] = dr
                    disp[slot, 3 + i, at, :] = di

    for g in range(slots * moms // per):
        for r in range(per):
            slot, p = divmod(g * per + r, moms)
            co = trig_ref[k, p : p + 1, :]
            si = trig_ref[k, moms + p : moms + p + 1, :]
            for i in range(3):
                dr, di = disp[slot, i], disp[slot, 3 + i]
                for part, value in ((0, co * dr + si * di), (1, co * di - si * dr)):
                    high, low = split(value)
                    first = part * half + i * LANES
                    dhi[g, r * cols : (r + 1) * cols, first : first + LANES] = high
                    dlo[g, r * cols : (r + 1) * cols, first : first + LANES] = low
        high, low = dhi[g], dlo[g]
        acc_ref[g * group : (g + 1) * group, :] += lax.dot_general(
            jnp.concatenate([high, high, low], axis=1),
            whole[...],
            (((1,), (1,)), ((), ())),
            preferred_element_type=jnp.float32,
        )

    @pl.when(k == kt - 1)
    def _():
        span = moms * cols
        for slot in range(slots):
            for part in range(2):
                block = acc_ref[slot * span : (slot + 1) * span, part * rows : (part + 1) * rows]
                first = (slot * 2 + part) * span
                turned[:, first : first + span] = norm * block.T
        part = rows // tiles
        for s in range(tiles):
            out_refs[s][...] = turned[pl.ds(pl.multiple_of(lax.rem(mine + s, tiles) * part, 8), part), :]


def along_tiles(value, steps):
    if steps == 0:
        return value
    count = lax.axis_size("tile")
    return lax.ppermute(value, "tile", [(i, (i + steps) % count) for i in range(count)])


def vec_cores():
    return 2 if lax.axis_size("vec") % 2 == 0 else 1


def over_chips(value):
    count = lax.axis_size("vec")
    blocks = [value]
    for step in range(vec_cores(), count, vec_cores()):
        blocks.append(lax.ppermute(value, "vec", [(i, (i + step) % count) for i in range(count)]))
    return blocks


def over_cores(blocks):
    if vec_cores() == 1:
        return []
    count = lax.axis_size("vec")
    return [lax.ppermute(block, "vec", [(i, i ^ 1) for i in range(count)]) for block in blocks]


def block_owners():
    count, here = lax.axis_size("vec"), lax.axis_index("vec")
    owner = [lax.rem(here - step + count, count) for step in range(0, count, vec_cores())]
    if vec_cores() == 2:
        owner += [other + 1 - 2 * (here % 2) for other in owner]
    return jnp.stack(owner).astype(jnp.int32)


def local(vectors, links, momenta, directions):
    nv = vectors.shape[1]
    sites = vectors.shape[3]
    tiles = lax.axis_size("tile")
    vecs = lax.axis_size("vec")
    tile = lax.axis_index("tile")
    slots = directions.shape[0]
    moms = momenta.shape[0]
    nvt = nv // tiles
    chunks = 2 if nvt % 16 == 0 else 1
    nvc = nvt // chunks
    kt = sites // LANES
    nt = kt * tiles
    extent_x = sites * tiles // PLANE
    norm = 1.0 / math.sqrt(3.0 * sites * tiles)
    f32 = jnp.float32
    smem = pl.BlockSpec(memory_space=pltpu.SMEM)
    vmem = pl.BlockSpec(memory_space=pltpu.VMEM)

    heading = directions % 3
    uses_y = jnp.any(heading == 1)
    uses_x = jnp.any(heading == 0)
    mode = jnp.where(uses_y, jnp.where(uses_x, 2, 0), 1).astype(jnp.int32)
    scal = jnp.concatenate([jnp.stack([mode, tile.astype(jnp.int32)]), directions.astype(jnp.int32)])

    parts = jnp.transpose(vectors, (0, 2, 1, 3)).reshape(6, tiles, chunks, nvc, sites)
    parts = jnp.transpose(parts, (2, 1, 0, 3, 4)).reshape(chunks, tiles, 6 * nvc, sites)
    share = sites // vecs
    link_share = lax.dynamic_slice_in_dim(links.reshape(54, sites), lax.axis_index("vec") * share, share, 1)
    gauge = lax.all_gather(link_share, ("vec", "tile"), axis=0).reshape(vecs, tiles, 54, share)
    fields = []
    for c in range(chunks):
        sent = [lax.dynamic_index_in_dim(parts[c], lax.rem(tile + s, tiles), 0, keepdims=False) for s in range(tiles)]
        if c > 0:
            for s in range(1, tiles):
                fields[c - 1][s], sent[s] = lax.optimization_barrier((fields[c - 1][s], sent[s]))
        fields.append([along_tiles(block, s) for s, block in enumerate(sent)])

    piece_shapes = (jax.ShapeDtypeStruct((kt, 6, nvc, LANES), f32),) * tiles
    link_shape = (6, nt, 18, LANES)
    owns, lefts = [], []
    for c in range(chunks):
        scratch = [pltpu.VMEM((nt, 6, nvc, LANES), f32)] * 2
        call = functools.partial(
            pl.pallas_call,
            functools.partial(filter_kernel, tiles, kt, nvc, c == 0),
            scratch_shapes=scratch,
            compiler_params=pltpu.CompilerParams(vmem_limit_bytes=48 << 20),
            cost_estimate=pl.CostEstimate(
                flops=250 * ITERS * 432 * nvc * nt * LANES, bytes_accessed=48 * nvc * nt * LANES, transcendentals=0
            ),
            name="chebyshev",
        )
        if c == 0:
            *pieces, glink, turned = call(
                out_shape=(
                    *piece_shapes,
                    jax.ShapeDtypeStruct((slots, kt, 18, LANES), f32),
                    jax.ShapeDtypeStruct(link_shape, f32),
                ),
                in_specs=[smem] + [vmem] * (tiles + 1),
                out_specs=(vmem,) * (tiles + 2),
            )(scal, *fields[c], gauge)
        else:
            pieces = call(out_shape=piece_shapes, in_specs=[smem] + [vmem] * (tiles + 1), out_specs=(vmem,) * tiles)(
                scal, *fields[c], turned
            )
        if c + 1 < chunks:
            fields[c + 1], pieces = lax.optimization_barrier((fields[c + 1], pieces))
        if c > 0:
            own, pieces = lax.optimization_barrier((own, pieces))
            owns[c - 1] = jnp.stack(own)
        own = [along_tiles(pieces[s], s) for s in range(tiles)]
        owns.append(jnp.stack(own))
    for c in range(chunks):
        if nvc % 8:
            owns[c] = owns[c][jnp.mod(tile - jnp.arange(tiles, dtype=jnp.int32), tiles)]
        lefts.append(over_chips(owns[c]))
        if c == 1:
            lefts[0][1:], owns[1] = lax.optimization_barrier((lefts[0][1:], owns[1]))
            lefts[1][0] = owns[1]
    owner = block_owners()

    k = jnp.arange(kt, dtype=jnp.int32)[:, None]
    lane = jnp.arange(LANES, dtype=jnp.int32)[None]

    def pick(options):
        return jnp.where(mode == 0, options[0], jnp.where(mode == 1, options[1], options[2]))

    coords = [piece_coords(m, tile, tiles, k, lane) for m in range(3)]
    x, y, z = (pick([jnp.broadcast_to(c[axis], (kt, LANES)) for c in coords]) for axis in range(3))
    start_x = jnp.where(mode == 0, tile * (sites // PLANE), 0)

    def part(axis, coord, extent):
        return jnp.mod(momenta[:, axis, None, None] * coord[None], extent).astype(f32) / extent

    angle = 2.0 * math.pi * (part(0, x + start_x, extent_x) + part(1, y, LY) + part(2, z, LZ))
    trig = jnp.transpose(jnp.concatenate([jnp.cos(angle), jnp.sin(angle)]), (1, 0, 2))

    index, spots = [], []
    for slot in range(slots):
        d = directions[slot]
        step = jnp.where(d < 3, 1, -1)
        xs = jnp.mod(x + jnp.where(heading[slot] == 0, step, 0), extent_x)
        ys = jnp.mod(y + jnp.where(heading[slot] == 1, step, 0), LY)
        zs = jnp.mod(z + jnp.where(heading[slot] == 2, step, 0), LZ)
        found = [piece_index(m, tile, tiles, xs, ys, zs) for m in range(3)]
        ks, ls = (pick([f[i] for f in found]) for i in range(2))
        ka, kb = jnp.min(ks, axis=1), jnp.max(ks, axis=1)
        index.append(jnp.stack([ls, (ks == kb[:, None]).astype(jnp.int32)], axis=1))
        spots.append(jnp.concatenate([ka, kb, (d < 3).astype(jnp.int32)[None]]))
    spots.append(jnp.broadcast_to(tile.astype(jnp.int32), spots[0].shape))
    spots.append(jnp.pad(owner, (0, 2 * kt + 1 - vecs)))
    index, spots = jnp.stack(index), jnp.stack(spots).astype(jnp.int32)

    rows, cols = vecs * tiles * nvc, nv
    depth = 6 * LANES
    group = cols * max(1, min(moms, 256 // cols))
    groups = slots * moms * cols // group
    bf16 = jnp.bfloat16
    mine = []
    for c in range(chunks):
        near, far = lefts[c][:1], lefts[c][1:]
        twins = over_cores(near)
        if c > 0:
            far, partial_rows = lax.optimization_barrier((far, partial_rows))
        left = near + far + twins + over_cores(far)
        if nvc % 8:
            left = list(jnp.stack(left)[jnp.argsort(owner)])
        if c > 0:
            mine.append(functools.reduce(jnp.add, [along_tiles(partial_rows[s], s) for s in range(tiles)]))
        partial_rows = pl.pallas_call(
            functools.partial(contract_kernel, vecs, chunks, slots, moms, norm),
            grid=(kt,),
            out_shape=(jax.ShapeDtypeStruct((rows // tiles, slots * 2 * moms * cols), f32),) * tiles,
            in_specs=[smem]
            + [pl.BlockSpec((tiles, 1, 6, nvc, LANES), lambda i: (0, i, 0, 0, 0))] * vecs
            + [vmem] * (chunks + 3),
            out_specs=(vmem,) * tiles,
            scratch_shapes=[
                pltpu.VMEM((rows, depth), f32),
                pltpu.VMEM((slots, 6, cols, LANES), f32),
                pltpu.VMEM((2 * rows, 3 * depth), bf16),
                pltpu.VMEM((groups, group, depth), bf16),
                pltpu.VMEM((groups, group, depth), bf16),
                pltpu.VMEM((slots * moms * cols, 2 * rows), f32),
                pltpu.VMEM((rows, slots * 2 * moms * cols), f32),
            ],
            compiler_params=pltpu.CompilerParams(vmem_limit_bytes=48 << 20),
            cost_estimate=pl.CostEstimate(
                flops=24 * rows * slots * moms * cols * 6 * sites, bytes_accessed=32 * rows * sites, transcendentals=0
            ),
            name="contract",
        )(spots, *left, *owns, trig, glink, index)
    mine.append(functools.reduce(jnp.add, [along_tiles(partial_rows[s], s) for s in range(tiles)]))
    mine = [m.reshape(-1, nvc, slots * 2 * moms * cols) for m in mine]
    return jnp.stack(mine, axis=1).reshape(nv * vecs // tiles, slots, 2, moms, cols)


def solution(mesh):
    return jax.shard_map(
        local,
        mesh=mesh,
        in_specs=(
            P(None, "vec", None, ("groups", "tile")),
            P(None, None, None, None, ("groups", "tile")),
            P(),
            P(),
        ),
        out_specs=P(("groups", "tile"), None, None, None, "vec"),
        check_vma=False,
    )
```

```python
import functools
import math

import jax
import jax.numpy as jnp
from jax import lax
from jax.experimental import pallas as pl
from jax.experimental.pallas import tpu as pltpu
from jax.sharding import PartitionSpec as P

LY = 16
LZ = 32
ITERS = 4
LANES = 128
PLANE = LY * LZ
QP = PLANE // LANES
YLO = LANES // LZ

hop_scale = 0.125


def piece_coords(mode, tile, tiles, k, lane):
    wy = (LY // tiles) * LZ
    bz = LZ // tiles
    if mode == 0:
        site = k * LANES + lane
        return site // PLANE, site % PLANE // LZ, site % LZ
    if mode == 1:
        flat = k * LANES + lane
        return flat // wy, tile * (LY // tiles) + flat % wy // LZ, lane % LZ
    slot = k * tiles + (lane % LZ) // bz
    return slot // QP, YLO * (slot % QP) + lane // LZ, tile * bz + lane % bz


def piece_index(mode, tile, tiles, x, y, z):
    wy = (LY // tiles) * LZ
    bz = LZ // tiles
    if mode == 0:
        site = x * PLANE + y * LZ + z
        return site // LANES, site % LANES
    if mode == 1:
        flat = x * wy + (y - tile * (LY // tiles)) * LZ + z
        return flat // LANES, flat % LANES
    slot = x * QP + y // YLO
    return slot // tiles, (y % YLO) * LZ + (slot % tiles) * bz + (z - tile * bz)


def pack_piece(mode, tiles, tile, read, write, kt):
    lane = lax.broadcasted_iota(jnp.int32, (1, LANES), 1)
    wy = (LY // tiles) * LZ
    bz = LZ // tiles

    def joined(indices, shifts, owner):
        out = None
        for j, (index, shift) in enumerate(zip(indices, shifts)):
            part = pltpu.roll(read(index), lax.rem(shift + 2 * LANES, LANES), 1)
            out = part if out is None else jnp.where(owner == j, part, out)
        return out

    def one(k, carry):
        if mode == 0:
            value = read(tile * kt + k)
        elif mode == 1 and wy >= LANES:
            per = wy // LANES
            value = read((k // per) * QP + tile * per + k % per)
        elif mode == 1:
            nx = LANES // wy
            first = k * nx * QP + (tile * wy) // LANES
            off = (tile * wy) % LANES
            value = joined([first + j * QP for j in range(nx)], [wy * j - off for j in range(nx)], lane // wy)
        else:
            shifts = [(j - tile) * bz for j in range(tiles)]
            value = joined([k * tiles + j for j in range(tiles)], shifts, (lane % LZ) // bz)
        write(k, value)
        return carry

    lax.fori_loop(0, kt, one, 0, unroll=tiles <= 4)


def filter_kernel(tiles, kt, rows, with_links, *refs):
    scal, slab_refs, refs = refs[0], refs[1 : 1 + tiles], refs[1 + tiles :]
    if with_links:
        link_ref, piece_refs, (glink_ref, l_ref, a_ref, b_ref) = refs[0], refs[1 : 1 + tiles], refs[1 + tiles :]
    else:
        l_ref, piece_refs, (a_ref, b_ref) = refs[0], refs[1 : 1 + tiles], refs[1 + tiles :]
    mine = scal[1]
    comps = 6
    nt = tiles * kt
    lx = nt // QP
    lane = lax.broadcasted_iota(jnp.int32, (1, LANES), 1)
    depth = lane % LZ

    def at(x, q):
        return x * QP + q

    def moved(get, x, q, axis, step):
        n = at(x, q)
        if axis == 0:
            return get(at(lax.rem(x + step + lx, lx), q))
        if axis == 1:
            here, there = get(n), get(at(x, (q + step) % QP))
            if step > 0:
                return rolled(jnp.where(lane < LZ, there, here), LANES - LZ)
            return rolled(jnp.where(lane >= LANES - LZ, there, here), LZ)
        here = get(n)
        if step > 0:
            return jnp.where(depth == LZ - 1, rolled(here, LZ - 1), rolled(here, LANES - 1))
        return jnp.where(depth == 0, rolled(here, LANES - LZ + 1), rolled(here, 1))

    def rolled(value, shift):
        return pltpu.roll(value, shift, value.ndim - 1)

    for s in range(tiles):
        t = lax.rem(mine - s + tiles, tiles)
        for k in range(kt):
            lanes = slice(k * LANES, (k + 1) * LANES)
            for c in range(comps):
                a_ref[t * kt + k, c] = slab_refs[s][c * rows : (c + 1) * rows, lanes]
            if with_links:
                share = link_ref.shape[3] // LANES
                lanes = slice(k % share * LANES, (k % share + 1) * LANES)
                for m in range(3):
                    l_ref[m, t * kt + k] = link_ref[k // share, s, 18 * m : 18 * m + 18, lanes]

    if with_links:

        def shift_links(x, carry):
            for q in range(QP):
                for m in range(3):
                    l_ref[3 + m, at(x, q)] = moved(lambda i: l_ref[m, i], x, q, m, -1)
            return carry

        lax.fori_loop(0, lx, shift_links, 0)

    def hop(src, x, q):
        n = at(x, q)
        acc = [None] * comps
        for m in range(3):
            for side in (0, 1):
                near = [moved(lambda i: src[i, c], x, q, m, 1 - 2 * side) for c in range(comps)]
                for i in range(3):
                    for j in range(3):
                        row = i * 3 + j if side == 0 else j * 3 + i
                        lr = l_ref[3 * side + m, n, row : row + 1, :]
                        li = l_ref[3 * side + m, n, 9 + row : 10 + row, :]
                        fr, fi = near[j], near[3 + j]
                        if side == 0:
                            re = lr * fr - li * fi
                            im = lr * fi + li * fr
                        else:
                            re = lr * fr + li * fi
                            im = lr * fi - li * fr
                        acc[i] = re if acc[i] is None else acc[i] + re
                        acc[3 + i] = im if acc[3 + i] is None else acc[3 + i] + im
        return acc

    src, dst = a_ref, b_ref
    for order in range(ITERS):

        def body(x, carry, src=src, dst=dst, order=order):
            for q in range(QP):
                n = x * QP + q
                acc = hop(src, x, q)
                for c in range(comps):
                    if order == 0:
                        dst[n, c] = hop_scale * acc[c]
                    else:
                        dst[n, c] = (2.0 * hop_scale) * acc[c] - dst[n, c]
            return carry

        lax.fori_loop(0, lx, body, 0)
        src, dst = dst, src

    for mode in range(3):

        @pl.when(scal[0] == mode)
        def _():
            for s in range(tiles):
                for c in range(comps):

                    def write(k, value, s=s, c=c):
                        piece_refs[s][k, c] = value

                    pack_piece(mode, tiles, lax.rem(mine + s, tiles), lambda n, c=c: src[n, c], write, kt)
            if with_links:
                for slot in range(glink_ref.shape[0]):

                    def write(k, value, slot=slot):
                        glink_ref[slot, k] = value

                    pack_piece(mode, tiles, mine, lambda n, slot=slot: l_ref[scal[2 + slot], n], write, kt)


def contract_kernel(vecs, chunks, slots, moms, norm, scal, *refs):
    left_refs, own_refs, refs = refs[:vecs], refs[vecs : vecs + chunks], refs[vecs + chunks :]
    tiles, nvc = own_refs[0].shape[0], own_refs[0].shape[3]
    (trig_ref, glink_ref, index_ref), out_refs, refs = refs[:3], refs[3 : 3 + tiles], refs[3 + tiles :]
    side, disp, whole, dhi, dlo, acc_ref, turned = refs
    k = pl.program_id(0)
    rows = vecs * tiles * nvc
    cols = tiles * nvc * chunks
    comps = 6
    kt = pl.num_programs(0)
    depth = comps * LANES
    group = dhi.shape[1]
    per = group // cols
    half = 3 * LANES

    mine = scal[slots, 0]

    def split(value):
        high = value.astype(jnp.bfloat16)
        return high, (value - high.astype(jnp.float32)).astype(jnp.bfloat16)

    def place(s, outer, count):
        if nvc % 8:
            return (outer * tiles + s) * count
        return pl.multiple_of((outer * tiles + lax.rem(mine - s + tiles, tiles)) * count, 8)

    @pl.when(k == 0)
    def _():
        acc_ref[...] = jnp.zeros_like(acc_ref)

    for v in range(vecs):
        for t in range(tiles):
            at = pl.ds(place(t, v if nvc % 8 else scal[slots + 1, v], nvc), nvc)
            for c in range(comps):
                side[at, c * LANES : (c + 1) * LANES] = left_refs[v][t, 0, c]
    for c in range(3):
        rh, rl = split(side[:, c * LANES : (c + 1) * LANES])
        ih, il = split(side[:, half + c * LANES : half + (c + 1) * LANES])
        for third, re, im in ((0, rh, ih), (1, rl, il), (2, rh, ih)):
            first = third * depth + c * LANES
            whole[0:rows, first : first + LANES] = re
            whole[0:rows, first + half : first + half + LANES] = im
            whole[rows : 2 * rows, first : first + LANES] = -im
            whole[rows : 2 * rows, first + half : first + half + LANES] = re

    for slot in range(slots):
        ka, kb = scal[slot, k], scal[slot, kt + k]
        forward = scal[slot, 2 * kt] > 0
        sign = jnp.where(forward, 1.0, -1.0)
        lanes = jnp.broadcast_to(index_ref[slot, k, 0:1, :], (nvc, LANES))
        take_b = jnp.broadcast_to(index_ref[slot, k, 1:2, :], (nvc, LANES)) > 0
        link = []
        for i in range(3):
            for j in range(3):
                row = jnp.where(forward, i * 3 + j, j * 3 + i)
                link.append((glink_ref[slot, k, pl.ds(row, 1), :], sign * glink_ref[slot, k, pl.ds(9 + row, 1), :]))
        for t in range(tiles):
            for part in range(chunks):
                near = []
                for c in range(comps):
                    first = jnp.take_along_axis(own_refs[part][t, ka, c], lanes, axis=1)
                    second = jnp.take_along_axis(own_refs[part][t, kb, c], lanes, axis=1)
                    near.append(jnp.where(take_b, second, first))
                at = pl.ds(place(t, 0, chunks * nvc) + part * nvc, nvc)
                for i in range(3):
                    dr, di = 0.0, 0.0
                    for j in range(3):
                        lr, li = link[i * 3 + j]
                        dr = dr + lr * near[j] - li * near[3 + j]
                        di = di + lr * near[3 + j] + li * near[j]
                    disp[slot, i, at, :] = dr
                    disp[slot, 3 + i, at, :] = di

    def twist(g):
        for r in range(per):
            slot, p = divmod(g * per + r, moms)
            co = trig_ref[k, p : p + 1, :]
            si = trig_ref[k, moms + p : moms + p + 1, :]
            for i in range(3):
                dr, di = disp[slot, i], disp[slot, 3 + i]
                for part, value in ((0, co * dr + si * di), (1, co * di - si * dr)):
                    high, low = split(value)
                    first = part * half + i * LANES
                    dhi[g, r * cols : (r + 1) * cols, first : first + LANES] = high
                    dlo[g, r * cols : (r + 1) * cols, first : first + LANES] = low

    def multiply(g):
        high, low = dhi[g], dlo[g]
        acc_ref[g * group : (g + 1) * group, :] += lax.dot_general(
            jnp.concatenate([high, high, low], axis=1),
            whole[...],
            (((1,), (1,)), ((), ())),
            preferred_element_type=jnp.float32,
        )

    groups = dhi.shape[0]
    twist(0)
    for g in range(groups):
        if g + 1 < groups:
            twist(g + 1)
        multiply(g)

    @pl.when(k == kt - 1)
    def _():
        span = moms * cols
        for slot in range(slots):
            for part in range(2):
                block = acc_ref[slot * span : (slot + 1) * span, part * rows : (part + 1) * rows]
                first = (slot * 2 + part) * span
                turned[:, first : first + span] = norm * block.T
        part = rows // tiles
        for s in range(tiles):
            out_refs[s][...] = turned[pl.ds(pl.multiple_of(lax.rem(mine + s, tiles) * part, 8), part), :]


def along_tiles(value, steps):
    if steps == 0:
        return value
    count = lax.axis_size("tile")
    return lax.ppermute(value, "tile", [(i, (i + steps) % count) for i in range(count)])


def vec_cores():
    return 2 if lax.axis_size("vec") % 2 == 0 else 1


def over_chips(value):
    count = lax.axis_size("vec")
    blocks = [value]
    for step in range(vec_cores(), count, vec_cores()):
        blocks.append(lax.ppermute(value, "vec", [(i, (i + step) % count) for i in range(count)]))
    return blocks


def over_cores(blocks):
    if vec_cores() == 1:
        return []
    count = lax.axis_size("vec")
    return [lax.ppermute(block, "vec", [(i, i ^ 1) for i in range(count)]) for block in blocks]


def block_owners():
    count, here = lax.axis_size("vec"), lax.axis_index("vec")
    owner = [lax.rem(here - step + count, count) for step in range(0, count, vec_cores())]
    if vec_cores() == 2:
        owner += [other + 1 - 2 * (here % 2) for other in owner]
    return jnp.stack(owner).astype(jnp.int32)


def local(vectors, links, momenta, directions):
    nv = vectors.shape[1]
    sites = vectors.shape[3]
    tiles = lax.axis_size("tile")
    vecs = lax.axis_size("vec")
    tile = lax.axis_index("tile")
    slots = directions.shape[0]
    moms = momenta.shape[0]
    nvt = nv // tiles
    chunks = 2 if nvt % 16 == 0 else 1
    nvc = nvt // chunks
    kt = sites // LANES
    nt = kt * tiles
    extent_x = sites * tiles // PLANE
    norm = 1.0 / math.sqrt(3.0 * sites * tiles)
    f32 = jnp.float32
    smem = pl.BlockSpec(memory_space=pltpu.SMEM)
    vmem = pl.BlockSpec(memory_space=pltpu.VMEM)

    heading = directions % 3
    uses_y = jnp.any(heading == 1)
    uses_x = jnp.any(heading == 0)
    mode = jnp.where(uses_y, jnp.where(uses_x, 2, 0), 1).astype(jnp.int32)
    scal = jnp.concatenate([jnp.stack([mode, tile.astype(jnp.int32)]), directions.astype(jnp.int32)])

    parts = jnp.transpose(vectors, (0, 2, 1, 3)).reshape(6, tiles, chunks, nvc, sites)
    parts = jnp.transpose(parts, (2, 1, 0, 3, 4)).reshape(chunks, tiles, 6 * nvc, sites)
    share = sites // vecs
    link_share = lax.dynamic_slice_in_dim(links.reshape(54, sites), lax.axis_index("vec") * share, share, 1)
    gauge = lax.all_gather(jnp.stack([along_tiles(link_share, s) for s in range(tiles)]), "vec", axis=0)
    fields = []
    for c in range(chunks):
        sent = [lax.dynamic_index_in_dim(parts[c], lax.rem(tile + s, tiles), 0, keepdims=False) for s in range(tiles)]
        if c > 0:
            for s in range(1, tiles):
                fields[c - 1][s], sent[s] = lax.optimization_barrier((fields[c - 1][s], sent[s]))
        fields.append([along_tiles(block, s) for s, block in enumerate(sent)])

    piece_shapes = (jax.ShapeDtypeStruct((kt, 6, nvc, LANES), f32),) * tiles
    link_shape = (6, nt, 18, LANES)
    owns, lefts = [], []
    for c in range(chunks):
        scratch = [pltpu.VMEM((nt, 6, nvc, LANES), f32)] * 2
        call = functools.partial(
            pl.pallas_call,
            functools.partial(filter_kernel, tiles, kt, nvc, c == 0),
            scratch_shapes=scratch,
            compiler_params=pltpu.CompilerParams(vmem_limit_bytes=48 << 20),
            cost_estimate=pl.CostEstimate(
                flops=250 * ITERS * 432 * nvc * nt * LANES, bytes_accessed=48 * nvc * nt * LANES, transcendentals=0
            ),
            name="chebyshev",
        )
        if c == 0:
            *pieces, glink, turned = call(
                out_shape=(
                    *piece_shapes,
                    jax.ShapeDtypeStruct((slots, kt, 18, LANES), f32),
                    jax.ShapeDtypeStruct(link_shape, f32),
                ),
                in_specs=[smem] + [vmem] * (tiles + 1),
                out_specs=(vmem,) * (tiles + 2),
            )(scal, *fields[c], gauge)
            glink, momenta, directions = lax.optimization_barrier((glink, momenta, directions))
            heading = directions % 3
        else:
            pieces = call(out_shape=piece_shapes, in_specs=[smem] + [vmem] * (tiles + 1), out_specs=(vmem,) * tiles)(
                scal, *fields[c], turned
            )
        if c + 1 < chunks:
            fields[c + 1], pieces = lax.optimization_barrier((fields[c + 1], pieces))
        if c > 0:
            own, pieces = lax.optimization_barrier((own, pieces))
            owns[c - 1] = jnp.stack(own)
        own = [along_tiles(pieces[s], s) for s in range(tiles)]
        owns.append(jnp.stack(own))
    for c in range(chunks):
        if nvc % 8:
            owns[c] = owns[c][jnp.mod(tile - jnp.arange(tiles, dtype=jnp.int32), tiles)]
        lefts.append(over_chips(owns[c]))
        if c == 1:
            lefts[0][1:], owns[1] = lax.optimization_barrier((lefts[0][1:], owns[1]))
            lefts[1][0] = owns[1]
    owner = block_owners()

    k = jnp.arange(kt, dtype=jnp.int32)[:, None]
    lane = jnp.arange(LANES, dtype=jnp.int32)[None]

    def pick(options):
        return jnp.where(mode == 0, options[0], jnp.where(mode == 1, options[1], options[2]))

    coords = [piece_coords(m, tile, tiles, k, lane) for m in range(3)]
    x, y, z = (pick([jnp.broadcast_to(c[axis], (kt, LANES)) for c in coords]) for axis in range(3))
    start_x = jnp.where(mode == 0, tile * (sites // PLANE), 0)

    def part(axis, coord, extent):
        return jnp.mod(momenta[:, axis, None, None] * coord[None], extent).astype(f32) / extent

    angle = 2.0 * math.pi * (part(0, x + start_x, extent_x) + part(1, y, LY) + part(2, z, LZ))
    trig = jnp.transpose(jnp.concatenate([jnp.cos(angle), jnp.sin(angle)]), (1, 0, 2))

    index, spots = [], []
    for slot in range(slots):
        d = directions[slot]
        step = jnp.where(d < 3, 1, -1)
        xs = jnp.mod(x + jnp.where(heading[slot] == 0, step, 0), extent_x)
        ys = jnp.mod(y + jnp.where(heading[slot] == 1, step, 0), LY)
        zs = jnp.mod(z + jnp.where(heading[slot] == 2, step, 0), LZ)
        found = [piece_index(m, tile, tiles, xs, ys, zs) for m in range(3)]
        ks, ls = (pick([f[i] for f in found]) for i in range(2))
        ka, kb = jnp.min(ks, axis=1), jnp.max(ks, axis=1)
        index.append(jnp.stack([ls, (ks == kb[:, None]).astype(jnp.int32)], axis=1))
        spots.append(jnp.concatenate([ka, kb, (d < 3).astype(jnp.int32)[None]]))
    spots.append(jnp.broadcast_to(tile.astype(jnp.int32), spots[0].shape))
    spots.append(jnp.pad(owner, (0, 2 * kt + 1 - vecs)))
    index, spots = jnp.stack(index), jnp.stack(spots).astype(jnp.int32)

    rows, cols = vecs * tiles * nvc, nv
    depth = 6 * LANES
    group = cols * max(1, min(moms, 256 // cols))
    groups = slots * moms * cols // group
    bf16 = jnp.bfloat16
    mine = []
    for c in range(chunks):
        near, far = lefts[c][:1], lefts[c][1:]
        twins = over_cores(near)
        if c > 0:
            far, partial_rows = lax.optimization_barrier((far, partial_rows))
        left = near + far + twins + over_cores(far)
        if nvc % 8:
            left = list(jnp.stack(left)[jnp.argsort(owner)])
        if c > 0:
            mine.append(functools.reduce(jnp.add, [along_tiles(partial_rows[s], s) for s in range(tiles)]))
        partial_rows = pl.pallas_call(
            functools.partial(contract_kernel, vecs, chunks, slots, moms, norm),
            grid=(kt,),
            out_shape=(jax.ShapeDtypeStruct((rows // tiles, slots * 2 * moms * cols), f32),) * tiles,
            in_specs=[smem]
            + [pl.BlockSpec((tiles, 1, 6, nvc, LANES), lambda i: (0, i, 0, 0, 0))] * vecs
            + [vmem] * (chunks + 3),
            out_specs=(vmem,) * tiles,
            scratch_shapes=[
                pltpu.VMEM((rows, depth), f32),
                pltpu.VMEM((slots, 6, cols, LANES), f32),
                pltpu.VMEM((2 * rows, 3 * depth), bf16),
                pltpu.VMEM((groups, group, depth), bf16),
                pltpu.VMEM((groups, group, depth), bf16),
                pltpu.VMEM((slots * moms * cols, 2 * rows), f32),
                pltpu.VMEM((rows, slots * 2 * moms * cols), f32),
            ],
            compiler_params=pltpu.CompilerParams(vmem_limit_bytes=48 << 20),
            cost_estimate=pl.CostEstimate(
                flops=24 * rows * slots * moms * cols * 6 * sites, bytes_accessed=32 * rows * sites, transcendentals=0
            ),
            name="contract",
        )(spots, *left, *owns, trig, glink, index)
    mine.append(functools.reduce(jnp.add, [along_tiles(partial_rows[s], s) for s in range(tiles)]))
    mine = [m.reshape(-1, nvc, slots * 2 * moms * cols) for m in mine]
    return jnp.stack(mine, axis=1).reshape(nv * vecs // tiles, slots, 2, moms, cols)


def solution(mesh):
    return jax.shard_map(
        local,
        mesh=mesh,
        in_specs=(
            P(None, "vec", None, ("groups", "tile")),
            P(None, None, None, None, ("groups", "tile")),
            P(),
            P(),
        ),
        out_specs=P(("groups", "tile"), None, None, None, "vec"),
        check_vma=False,
    )
```

```python
import functools
import math

import jax
import jax.numpy as jnp
from jax import lax
from jax.experimental import pallas as pl
from jax.experimental.pallas import tpu as pltpu
from jax.sharding import PartitionSpec as P

LY = 16
LZ = 32
ITERS = 4
LANES = 128
PLANE = LY * LZ
QP = PLANE // LANES
YLO = LANES // LZ

hop_scale = 0.125


def piece_coords(mode, tile, tiles, k, lane):
    wy = (LY // tiles) * LZ
    bz = LZ // tiles
    if mode == 0:
        site = k * LANES + lane
        return site // PLANE, site % PLANE // LZ, site % LZ
    if mode == 1:
        flat = k * LANES + lane
        return flat // wy, tile * (LY // tiles) + flat % wy // LZ, lane % LZ
    slot = k * tiles + (lane % LZ) // bz
    return slot // QP, YLO * (slot % QP) + lane // LZ, tile * bz + lane % bz


def piece_index(mode, tile, tiles, x, y, z):
    wy = (LY // tiles) * LZ
    bz = LZ // tiles
    if mode == 0:
        site = x * PLANE + y * LZ + z
        return site // LANES, site % LANES
    if mode == 1:
        flat = x * wy + (y - tile * (LY // tiles)) * LZ + z
        return flat // LANES, flat % LANES
    slot = x * QP + y // YLO
    return slot // tiles, (y % YLO) * LZ + (slot % tiles) * bz + (z - tile * bz)


def pack_piece(mode, tiles, tile, read, write, kt):
    lane = lax.broadcasted_iota(jnp.int32, (1, LANES), 1)
    wy = (LY // tiles) * LZ
    bz = LZ // tiles

    def joined(indices, shifts, owner):
        out = None
        for j, (index, shift) in enumerate(zip(indices, shifts)):
            part = pltpu.roll(read(index), lax.rem(shift + 2 * LANES, LANES), 1)
            out = part if out is None else jnp.where(owner == j, part, out)
        return out

    def one(k, carry):
        if mode == 0:
            value = read(tile * kt + k)
        elif mode == 1 and wy >= LANES:
            per = wy // LANES
            value = read((k // per) * QP + tile * per + k % per)
        elif mode == 1:
            nx = LANES // wy
            first = k * nx * QP + (tile * wy) // LANES
            off = (tile * wy) % LANES
            value = joined([first + j * QP for j in range(nx)], [wy * j - off for j in range(nx)], lane // wy)
        else:
            shifts = [(j - tile) * bz for j in range(tiles)]
            value = joined([k * tiles + j for j in range(tiles)], shifts, (lane % LZ) // bz)
        write(k, value)
        return carry

    lax.fori_loop(0, kt, one, 0, unroll=tiles <= 4)


def filter_kernel(tiles, kt, rows, with_links, *refs):
    scal, slab_refs, refs = refs[0], refs[1 : 1 + tiles], refs[1 + tiles :]
    if with_links:
        link_ref, piece_refs, (glink_ref, l_ref, a_ref, b_ref) = refs[0], refs[1 : 1 + tiles], refs[1 + tiles :]
    else:
        l_ref, piece_refs, (a_ref, b_ref) = refs[0], refs[1 : 1 + tiles], refs[1 + tiles :]
    mine = scal[1]
    comps = 6
    nt = tiles * kt
    lx = nt // QP
    lane = lax.broadcasted_iota(jnp.int32, (1, LANES), 1)
    depth = lane % LZ

    def at(x, q):
        return x * QP + q

    def moved(get, x, q, axis, step):
        n = at(x, q)
        if axis == 0:
            return get(at(lax.rem(x + step + lx, lx), q))
        if axis == 1:
            here, there = get(n), get(at(x, (q + step) % QP))
            if step > 0:
                return rolled(jnp.where(lane < LZ, there, here), LANES - LZ)
            return rolled(jnp.where(lane >= LANES - LZ, there, here), LZ)
        here = get(n)
        if step > 0:
            return jnp.where(depth == LZ - 1, rolled(here, LZ - 1), rolled(here, LANES - 1))
        return jnp.where(depth == 0, rolled(here, LANES - LZ + 1), rolled(here, 1))

    def rolled(value, shift):
        return pltpu.roll(value, shift, value.ndim - 1)

    for s in range(tiles):
        t = lax.rem(mine - s + tiles, tiles)
        for k in range(kt):
            lanes = slice(k * LANES, (k + 1) * LANES)
            for c in range(comps):
                a_ref[t * kt + k, c] = slab_refs[s][c * rows : (c + 1) * rows, lanes]
            if with_links:
                share = link_ref.shape[3] // LANES
                lanes = slice(k % share * LANES, (k % share + 1) * LANES)
                for m in range(3):
                    l_ref[m, t * kt + k] = link_ref[k // share, s, 18 * m : 18 * m + 18, lanes]

    if with_links:

        def shift_links(x, carry):
            for q in range(QP):
                for m in range(3):
                    l_ref[3 + m, at(x, q)] = moved(lambda i: l_ref[m, i], x, q, m, -1)
            return carry

        lax.fori_loop(0, lx, shift_links, 0)

    def hop(src, x, q):
        n = at(x, q)
        acc = [None] * comps
        for m in range(3):
            for side in (0, 1):
                near = [moved(lambda i: src[i, c], x, q, m, 1 - 2 * side) for c in range(comps)]
                for i in range(3):
                    for j in range(3):
                        row = i * 3 + j if side == 0 else j * 3 + i
                        lr = l_ref[3 * side + m, n, row : row + 1, :]
                        li = l_ref[3 * side + m, n, 9 + row : 10 + row, :]
                        fr, fi = near[j], near[3 + j]
                        if side == 0:
                            re = lr * fr - li * fi
                            im = lr * fi + li * fr
                        else:
                            re = lr * fr + li * fi
                            im = lr * fi - li * fr
                        acc[i] = re if acc[i] is None else acc[i] + re
                        acc[3 + i] = im if acc[3 + i] is None else acc[3 + i] + im
        return acc

    src, dst = a_ref, b_ref
    for order in range(ITERS):

        def body(x, carry, src=src, dst=dst, order=order):
            for q in range(QP):
                n = x * QP + q
                acc = hop(src, x, q)
                for c in range(comps):
                    if order == 0:
                        dst[n, c] = hop_scale * acc[c]
                    else:
                        dst[n, c] = (2.0 * hop_scale) * acc[c] - dst[n, c]
            return carry

        lax.fori_loop(0, lx, body, 0)
        src, dst = dst, src

    for mode in range(3):

        @pl.when(scal[0] == mode)
        def _():
            for s in range(tiles):
                for c in range(comps):

                    def write(k, value, s=s, c=c):
                        piece_refs[s][k, c] = value

                    pack_piece(mode, tiles, lax.rem(mine + s, tiles), lambda n, c=c: src[n, c], write, kt)
            if with_links:
                for slot in range(glink_ref.shape[0]):

                    def write(k, value, slot=slot):
                        glink_ref[slot, k] = value

                    pack_piece(mode, tiles, mine, lambda n, slot=slot: l_ref[scal[2 + slot], n], write, kt)


def contract_kernel(vecs, chunks, slots, moms, norm, scal, *refs):
    left_refs, own_refs, refs = refs[:vecs], refs[vecs : vecs + chunks], refs[vecs + chunks :]
    tiles, nvc = own_refs[0].shape[0], own_refs[0].shape[3]
    (trig_ref, glink_ref, index_ref), out_refs, refs = refs[:3], refs[3 : 3 + tiles], refs[3 + tiles :]
    side, disp, whole, dhi, dlo, acc_ref, turned = refs
    k = pl.program_id(0)
    rows = vecs * tiles * nvc
    cols = tiles * nvc * chunks
    comps = 6
    kt = pl.num_programs(0)
    depth = comps * LANES
    half = 3 * LANES

    mine = scal[slots, 0]

    def split(value):
        high = value.astype(jnp.bfloat16)
        return high, (value - high.astype(jnp.float32)).astype(jnp.bfloat16)

    def place(s, outer, count):
        if nvc % 8:
            return (outer * tiles + s) * count
        return pl.multiple_of((outer * tiles + lax.rem(mine - s + tiles, tiles)) * count, 8)

    @pl.when(k == 0)
    def _():
        acc_ref[...] = jnp.zeros_like(acc_ref)

    for v in range(vecs):
        for t in range(tiles):
            at = pl.ds(place(t, v if nvc % 8 else scal[slots + 1, v], nvc), nvc)
            for c in range(comps):
                side[at, c * LANES : (c + 1) * LANES] = left_refs[v][t, 0, c]
    for c in range(3):
        rh, rl = split(side[:, c * LANES : (c + 1) * LANES].T)
        ih, il = split(side[:, half + c * LANES : half + (c + 1) * LANES].T)
        for third, re, im in ((0, rh, ih), (1, rl, il), (2, rh, ih)):
            first = third * depth + c * LANES
            whole[first : first + LANES, 0:rows] = re
            whole[first + half : first + half + LANES, 0:rows] = im
            whole[first : first + LANES, rows : 2 * rows] = -im
            whole[first + half : first + half + LANES, rows : 2 * rows] = re

    for slot in range(slots):
        ka, kb = scal[slot, k], scal[slot, kt + k]
        forward = scal[slot, 2 * kt] > 0
        sign = jnp.where(forward, 1.0, -1.0)
        lanes = jnp.broadcast_to(index_ref[slot, k, 0:1, :], (nvc, LANES))
        take_b = jnp.broadcast_to(index_ref[slot, k, 1:2, :], (nvc, LANES)) > 0
        link = []
        for i in range(3):
            for j in range(3):
                row = jnp.where(forward, i * 3 + j, j * 3 + i)
                link.append((glink_ref[slot, k, pl.ds(row, 1), :], sign * glink_ref[slot, k, pl.ds(9 + row, 1), :]))
        for t in range(tiles):
            for part in range(chunks):
                near = []
                for c in range(comps):
                    first = jnp.take_along_axis(own_refs[part][t, ka, c], lanes, axis=1)
                    second = jnp.take_along_axis(own_refs[part][t, kb, c], lanes, axis=1)
                    near.append(jnp.where(take_b, second, first))
                at = pl.ds(place(t, 0, chunks * nvc) + part * nvc, nvc)
                for i in range(3):
                    dr, di = 0.0, 0.0
                    for j in range(3):
                        lr, li = link[i * 3 + j]
                        dr = dr + lr * near[j] - li * near[3 + j]
                        di = di + lr * near[3 + j] + li * near[j]
                    disp[slot, i, at, :] = dr
                    disp[slot, 3 + i, at, :] = di

    for r in range(slots * moms):
        slot, p = divmod(r, moms)
        co = trig_ref[k, p : p + 1, :]
        si = trig_ref[k, moms + p : moms + p + 1, :]
        for i in range(3):
            dr, di = disp[slot, i], disp[slot, 3 + i]
            for part, value in ((0, co * dr + si * di), (1, co * di - si * dr)):
                high, low = split(value)
                first = part * half + i * LANES
                dhi[r * cols : (r + 1) * cols, first : first + LANES] = high
                dlo[r * cols : (r + 1) * cols, first : first + LANES] = low
    acc_ref[...] += jnp.dot(
        jnp.concatenate([dhi[...], dhi[...], dlo[...]], axis=1), whole[...], preferred_element_type=jnp.float32
    )

    @pl.when(k == kt - 1)
    def _():
        span = moms * cols
        for slot in range(slots):
            for part in range(2):
                block = acc_ref[slot * span : (slot + 1) * span, part * rows : (part + 1) * rows]
                first = (slot * 2 + part) * span
                turned[:, first : first + span] = norm * block.T
        part = rows // tiles
        for s in range(tiles):
            out_refs[s][...] = turned[pl.ds(pl.multiple_of(lax.rem(mine + s, tiles) * part, 8), part), :]


def along_tiles(value, steps):
    if steps == 0:
        return value
    count = lax.axis_size("tile")
    return lax.ppermute(value, "tile", [(i, (i + steps) % count) for i in range(count)])


def vec_cores():
    return 2 if lax.axis_size("vec") % 2 == 0 else 1


def over_chips(value):
    count = lax.axis_size("vec")
    blocks = [value]
    for step in range(vec_cores(), count, vec_cores()):
        blocks.append(lax.ppermute(value, "vec", [(i, (i + step) % count) for i in range(count)]))
    return blocks


def over_cores(blocks):
    if vec_cores() == 1:
        return []
    count = lax.axis_size("vec")
    return [lax.ppermute(block, "vec", [(i, i ^ 1) for i in range(count)]) for block in blocks]


def block_owners():
    count, here = lax.axis_size("vec"), lax.axis_index("vec")
    owner = [lax.rem(here - step + count, count) for step in range(0, count, vec_cores())]
    if vec_cores() == 2:
        owner += [other + 1 - 2 * (here % 2) for other in owner]
    return jnp.stack(owner).astype(jnp.int32)


def local(vectors, links, momenta, directions):
    nv = vectors.shape[1]
    sites = vectors.shape[3]
    tiles = lax.axis_size("tile")
    vecs = lax.axis_size("vec")
    tile = lax.axis_index("tile")
    slots = directions.shape[0]
    moms = momenta.shape[0]
    nvt = nv // tiles
    chunks = 2 if nvt % 16 == 0 else 1
    nvc = nvt // chunks
    kt = sites // LANES
    nt = kt * tiles
    extent_x = sites * tiles // PLANE
    norm = 1.0 / math.sqrt(3.0 * sites * tiles)
    f32 = jnp.float32
    smem = pl.BlockSpec(memory_space=pltpu.SMEM)
    vmem = pl.BlockSpec(memory_space=pltpu.VMEM)

    heading = directions % 3
    uses_y = jnp.any(heading == 1)
    uses_x = jnp.any(heading == 0)
    mode = jnp.where(uses_y, jnp.where(uses_x, 2, 0), 1).astype(jnp.int32)
    scal = jnp.concatenate([jnp.stack([mode, tile.astype(jnp.int32)]), directions.astype(jnp.int32)])

    parts = jnp.transpose(vectors, (0, 2, 1, 3)).reshape(6, tiles, chunks, nvc, sites)
    parts = jnp.transpose(parts, (2, 1, 0, 3, 4)).reshape(chunks, tiles, 6 * nvc, sites)
    share = sites // vecs
    link_share = lax.dynamic_slice_in_dim(links.reshape(54, sites), lax.axis_index("vec") * share, share, 1)
    shares = [along_tiles(link_share, s) for s in range(tiles)]
    shares, momenta, directions = lax.optimization_barrier((shares, momenta, directions))
    heading = directions % 3
    gauge = lax.all_gather(jnp.stack(shares), "vec", axis=0)
    fields = []
    for c in range(chunks):
        sent = [lax.dynamic_index_in_dim(parts[c], lax.rem(tile + s, tiles), 0, keepdims=False) for s in range(tiles)]
        if c > 0:
            fields[c - 1], sent = lax.optimization_barrier((fields[c - 1], sent))
        fields.append([along_tiles(block, s) for s, block in enumerate(sent)])

    k = jnp.arange(kt, dtype=jnp.int32)[:, None]
    lane = jnp.arange(LANES, dtype=jnp.int32)[None]

    def pick(options):
        return jnp.where(mode == 0, options[0], jnp.where(mode == 1, options[1], options[2]))

    coords = [piece_coords(m, tile, tiles, k, lane) for m in range(3)]
    x, y, z = (pick([jnp.broadcast_to(c[axis], (kt, LANES)) for c in coords]) for axis in range(3))
    start_x = jnp.where(mode == 0, tile * (sites // PLANE), 0)

    def part(axis, coord, extent):
        return jnp.mod(momenta[:, axis, None, None] * coord[None], extent).astype(f32) / extent

    angle = 2.0 * math.pi * (part(0, x + start_x, extent_x) + part(1, y, LY) + part(2, z, LZ))
    trig = jnp.transpose(jnp.concatenate([jnp.cos(angle), jnp.sin(angle)]), (1, 0, 2))

    index, spots = [], []
    for slot in range(slots):
        d = directions[slot]
        step = jnp.where(d < 3, 1, -1)
        xs = jnp.mod(x + jnp.where(heading[slot] == 0, step, 0), extent_x)
        ys = jnp.mod(y + jnp.where(heading[slot] == 1, step, 0), LY)
        zs = jnp.mod(z + jnp.where(heading[slot] == 2, step, 0), LZ)
        found = [piece_index(m, tile, tiles, xs, ys, zs) for m in range(3)]
        ks, ls = (pick([f[i] for f in found]) for i in range(2))
        ka, kb = jnp.min(ks, axis=1), jnp.max(ks, axis=1)
        index.append(jnp.stack([ls, (ks == kb[:, None]).astype(jnp.int32)], axis=1))
        spots.append(jnp.concatenate([ka, kb, (d < 3).astype(jnp.int32)[None]]))
    owner = block_owners()
    spots.append(jnp.broadcast_to(tile.astype(jnp.int32), spots[0].shape))
    spots.append(jnp.pad(owner, (0, 2 * kt + 1 - vecs)))
    index, spots = jnp.stack(index), jnp.stack(spots).astype(jnp.int32)

    fields[0][0], trig, index, spots = lax.optimization_barrier((fields[0][0], trig, index, spots))

    piece_shapes = (jax.ShapeDtypeStruct((kt, 6, nvc, LANES), f32),) * tiles
    link_shape = (6, nt, 18, LANES)
    owns, lefts = [], []
    for c in range(chunks):
        scratch = [pltpu.VMEM((nt, 6, nvc, LANES), f32)] * 2
        call = functools.partial(
            pl.pallas_call,
            functools.partial(filter_kernel, tiles, kt, nvc, c == 0),
            scratch_shapes=scratch,
            compiler_params=pltpu.CompilerParams(vmem_limit_bytes=48 << 20),
            cost_estimate=pl.CostEstimate(
                flops=250 * ITERS * 432 * nvc * nt * LANES, bytes_accessed=48 * nvc * nt * LANES, transcendentals=0
            ),
            name="chebyshev",
        )
        if c == 0:
            *pieces, glink, turned = call(
                out_shape=(
                    *piece_shapes,
                    jax.ShapeDtypeStruct((slots, kt, 18, LANES), f32),
                    jax.ShapeDtypeStruct(link_shape, f32),
                ),
                in_specs=[smem] + [vmem] * (tiles + 1),
                out_specs=(vmem,) * (tiles + 2),
            )(scal, *fields[c], gauge)
        else:
            pieces = call(out_shape=piece_shapes, in_specs=[smem] + [vmem] * (tiles + 1), out_specs=(vmem,) * tiles)(
                scal, *fields[c], turned
            )
        if c + 1 < chunks:
            fields[c + 1], pieces = lax.optimization_barrier((fields[c + 1], pieces))
        if c > 0:
            own, pieces = lax.optimization_barrier((own, pieces))
            owns[c - 1] = jnp.stack(own)
        own = [along_tiles(pieces[s], s) for s in range(tiles)]
        owns.append(jnp.stack(own))
    for c in range(chunks):
        if nvc % 8:
            owns[c] = owns[c][jnp.mod(tile - jnp.arange(tiles, dtype=jnp.int32), tiles)]
        lefts.append(over_chips(owns[c]))
        if c == 1:
            lefts[0][1:], owns[1] = lax.optimization_barrier((lefts[0][1:], owns[1]))
            lefts[1][0] = owns[1]

    rows, cols = vecs * tiles * nvc, nv
    depth = 6 * LANES
    bf16 = jnp.bfloat16
    mine = []
    for c in range(chunks):
        near, far = lefts[c][:1], lefts[c][1:]
        twins = over_cores(near)
        if c > 0:
            far, partial_rows = lax.optimization_barrier((far, partial_rows))
        left = near + far + twins + over_cores(far)
        if nvc % 8:
            left = list(jnp.stack(left)[jnp.argsort(owner)])
        if c > 0:
            mine.append(functools.reduce(jnp.add, [along_tiles(partial_rows[s], s) for s in range(tiles)]))
        partial_rows = pl.pallas_call(
            functools.partial(contract_kernel, vecs, chunks, slots, moms, norm),
            grid=(kt,),
            out_shape=(jax.ShapeDtypeStruct((rows // tiles, slots * 2 * moms * cols), f32),) * tiles,
            in_specs=[smem]
            + [pl.BlockSpec((tiles, 1, 6, nvc, LANES), lambda i: (0, i, 0, 0, 0))] * vecs
            + [vmem] * (chunks + 3),
            out_specs=(vmem,) * tiles,
            scratch_shapes=[
                pltpu.VMEM((rows, depth), f32),
                pltpu.VMEM((slots, 6, cols, LANES), f32),
                pltpu.VMEM((3 * depth, 2 * rows), bf16),
                pltpu.VMEM((slots * moms * cols, depth), bf16),
                pltpu.VMEM((slots * moms * cols, depth), bf16),
                pltpu.VMEM((slots * moms * cols, 2 * rows), f32),
                pltpu.VMEM((rows, slots * 2 * moms * cols), f32),
            ],
            compiler_params=pltpu.CompilerParams(vmem_limit_bytes=48 << 20),
            cost_estimate=pl.CostEstimate(
                flops=24 * rows * slots * moms * cols * 6 * sites, bytes_accessed=32 * rows * sites, transcendentals=0
            ),
            name="contract",
        )(spots, *left, *owns, trig, glink, index)
    mine.append(functools.reduce(jnp.add, [along_tiles(partial_rows[s], s) for s in range(tiles)]))
    mine = [m.reshape(-1, nvc, slots * 2 * moms * cols) for m in mine]
    return jnp.stack(mine, axis=1).reshape(nv * vecs // tiles, slots, 2, moms, cols)


def solution(mesh):
    return jax.shard_map(
        local,
        mesh=mesh,
        in_specs=(
            P(None, "vec", None, ("groups", "tile")),
            P(None, None, None, None, ("groups", "tile")),
            P(),
            P(),
        ),
        out_specs=P(("groups", "tile"), None, None, None, "vec"),
        check_vma=False,
    )
```

```python
import functools
import math

import jax
import jax.numpy as jnp
from jax import lax
from jax.experimental import pallas as pl
from jax.experimental.pallas import tpu as pltpu
from jax.sharding import PartitionSpec as P

LY = 16
LZ = 32
ITERS = 4
LANES = 128
PLANE = LY * LZ
QP = PLANE // LANES
YLO = LANES // LZ

hop_scale = 0.125


def piece_coords(mode, tile, tiles, k, lane):
    wy = (LY // tiles) * LZ
    bz = LZ // tiles
    if mode == 0:
        site = k * LANES + lane
        return site // PLANE, site % PLANE // LZ, site % LZ
    if mode == 1:
        flat = k * LANES + lane
        return flat // wy, tile * (LY // tiles) + flat % wy // LZ, lane % LZ
    slot = k * tiles + (lane % LZ) // bz
    return slot // QP, YLO * (slot % QP) + lane // LZ, tile * bz + lane % bz


def piece_index(mode, tile, tiles, x, y, z):
    wy = (LY // tiles) * LZ
    bz = LZ // tiles
    if mode == 0:
        site = x * PLANE + y * LZ + z
        return site // LANES, site % LANES
    if mode == 1:
        flat = x * wy + (y - tile * (LY // tiles)) * LZ + z
        return flat // LANES, flat % LANES
    slot = x * QP + y // YLO
    return slot // tiles, (y % YLO) * LZ + (slot % tiles) * bz + (z - tile * bz)


def pack_piece(mode, tiles, tile, read, write, kt):
    lane = lax.broadcasted_iota(jnp.int32, (1, LANES), 1)
    wy = (LY // tiles) * LZ
    bz = LZ // tiles

    def joined(indices, shifts, owner):
        out = None
        for j, (index, shift) in enumerate(zip(indices, shifts)):
            part = pltpu.roll(read(index), lax.rem(shift + 2 * LANES, LANES), 1)
            out = part if out is None else jnp.where(owner == j, part, out)
        return out

    def one(k, carry):
        if mode == 0:
            value = read(tile * kt + k)
        elif mode == 1 and wy >= LANES:
            per = wy // LANES
            value = read((k // per) * QP + tile * per + k % per)
        elif mode == 1:
            nx = LANES // wy
            first = k * nx * QP + (tile * wy) // LANES
            off = (tile * wy) % LANES
            value = joined([first + j * QP for j in range(nx)], [wy * j - off for j in range(nx)], lane // wy)
        else:
            shifts = [(j - tile) * bz for j in range(tiles)]
            value = joined([k * tiles + j for j in range(tiles)], shifts, (lane % LZ) // bz)
        write(k, value)
        return carry

    lax.fori_loop(0, kt, one, 0, unroll=tiles <= 4)


def filter_kernel(tiles, kt, rows, with_links, *refs):
    scal, slab_refs, refs = refs[0], refs[1 : 1 + tiles], refs[1 + tiles :]
    if with_links:
        link_ref, piece_refs, (glink_ref, l_ref, a_ref, b_ref) = refs[0], refs[1 : 1 + tiles], refs[1 + tiles :]
    else:
        l_ref, piece_refs, (a_ref, b_ref) = refs[0], refs[1 : 1 + tiles], refs[1 + tiles :]
    mine = scal[1]
    comps = 6
    nt = tiles * kt
    lx = nt // QP
    lane = lax.broadcasted_iota(jnp.int32, (1, LANES), 1)
    depth = lane % LZ

    def at(x, q):
        return x * QP + q

    def moved(get, x, q, axis, step):
        n = at(x, q)
        if axis == 0:
            return get(at(lax.rem(x + step + lx, lx), q))
        if axis == 1:
            here, there = get(n), get(at(x, (q + step) % QP))
            if step > 0:
                return rolled(jnp.where(lane < LZ, there, here), LANES - LZ)
            return rolled(jnp.where(lane >= LANES - LZ, there, here), LZ)
        here = get(n)
        if step > 0:
            return jnp.where(depth == LZ - 1, rolled(here, LZ - 1), rolled(here, LANES - 1))
        return jnp.where(depth == 0, rolled(here, LANES - LZ + 1), rolled(here, 1))

    def rolled(value, shift):
        return pltpu.roll(value, shift, value.ndim - 1)

    for s in range(tiles):
        t = lax.rem(mine - s + tiles, tiles)
        for k in range(kt):
            lanes = slice(k * LANES, (k + 1) * LANES)
            for c in range(comps):
                a_ref[t * kt + k, c] = slab_refs[s][c * rows : (c + 1) * rows, lanes]
            if with_links:
                share = link_ref.shape[3] // LANES
                lanes = slice(k % share * LANES, (k % share + 1) * LANES)
                for m in range(3):
                    l_ref[m, t * kt + k] = link_ref[k // share, s, 18 * m : 18 * m + 18, lanes]

    if with_links:

        def shift_links(x, carry):
            for q in range(QP):
                for m in range(3):
                    l_ref[3 + m, at(x, q)] = moved(lambda i: l_ref[m, i], x, q, m, -1)
            return carry

        lax.fori_loop(0, lx, shift_links, 0)

    def hop(src, x, q):
        n = at(x, q)
        acc = [None] * comps
        for m in range(3):
            for side in (0, 1):
                near = [moved(lambda i: src[i, c], x, q, m, 1 - 2 * side) for c in range(comps)]
                for i in range(3):
                    for j in range(3):
                        row = i * 3 + j if side == 0 else j * 3 + i
                        lr = l_ref[3 * side + m, n, row : row + 1, :]
                        li = l_ref[3 * side + m, n, 9 + row : 10 + row, :]
                        fr, fi = near[j], near[3 + j]
                        if side == 0:
                            re = lr * fr - li * fi
                            im = lr * fi + li * fr
                        else:
                            re = lr * fr + li * fi
                            im = lr * fi - li * fr
                        acc[i] = re if acc[i] is None else acc[i] + re
                        acc[3 + i] = im if acc[3 + i] is None else acc[3 + i] + im
        return acc

    src, dst = a_ref, b_ref
    for order in range(ITERS):

        def body(x, carry, src=src, dst=dst, order=order):
            for q in range(QP):
                n = x * QP + q
                acc = hop(src, x, q)
                for c in range(comps):
                    if order == 0:
                        dst[n, c] = hop_scale * acc[c]
                    else:
                        dst[n, c] = (2.0 * hop_scale) * acc[c] - dst[n, c]
            return carry

        lax.fori_loop(0, lx, body, 0)
        src, dst = dst, src

    for mode in range(3):

        @pl.when(scal[0] == mode)
        def _():
            for s in range(tiles):
                for c in range(comps):

                    def write(k, value, s=s, c=c):
                        piece_refs[s][k, c] = value

                    pack_piece(mode, tiles, lax.rem(mine + s, tiles), lambda n, c=c: src[n, c], write, kt)
            if with_links:
                for slot in range(glink_ref.shape[0]):

                    def write(k, value, slot=slot):
                        glink_ref[slot, k] = value

                    pack_piece(mode, tiles, mine, lambda n, slot=slot: l_ref[scal[2 + slot], n], write, kt)


def contract_kernel(vecs, chunks, slots, moms, norm, scal, *refs):
    left_refs, own_refs, refs = refs[:vecs], refs[vecs : vecs + chunks], refs[vecs + chunks :]
    tiles, nvc = own_refs[0].shape[0], own_refs[0].shape[3]
    (trig_ref, glink_ref, index_ref), out_refs, refs = refs[:3], refs[3 : 3 + tiles], refs[3 + tiles :]
    side, disp, whole, dhi, dlo, acc_ref, turned = refs
    k = pl.program_id(0)
    rows = vecs * tiles * nvc
    cols = tiles * nvc * chunks
    comps = 6
    kt = pl.num_programs(0)
    depth = comps * LANES
    half = 3 * LANES

    mine = scal[slots, 0]

    def split(value):
        high = value.astype(jnp.bfloat16)
        return high, (value - high.astype(jnp.float32)).astype(jnp.bfloat16)

    def place(s, outer, count):
        if nvc % 8:
            return (outer * tiles + s) * count
        return pl.multiple_of((outer * tiles + lax.rem(mine - s + tiles, tiles)) * count, 8)

    @pl.when(k == 0)
    def _():
        acc_ref[...] = jnp.zeros_like(acc_ref)

    for v in range(vecs):
        for t in range(tiles):
            at = pl.ds(place(t, v if nvc % 8 else scal[slots + 1, v], nvc), nvc)
            for c in range(comps):
                side[at, c * LANES : (c + 1) * LANES] = left_refs[v][t, 0, c]
    for c in range(3):
        rh, rl = split(side[:, c * LANES : (c + 1) * LANES].T)
        ih, il = split(side[:, half + c * LANES : half + (c + 1) * LANES].T)
        for third, re, im in ((0, rh, ih), (1, rl, il), (2, rh, ih)):
            first = third * depth + c * LANES
            whole[first : first + LANES, 0:rows] = re
            whole[first + half : first + half + LANES, 0:rows] = im
            whole[first : first + LANES, rows : 2 * rows] = -im
            whole[first + half : first + half + LANES, rows : 2 * rows] = re

    for slot in range(slots):
        ka, kb = scal[slot, k], scal[slot, kt + k]
        forward = scal[slot, 2 * kt] > 0
        sign = jnp.where(forward, 1.0, -1.0)
        lanes = jnp.broadcast_to(index_ref[slot, k, 0:1, :], (nvc, LANES))
        take_b = jnp.broadcast_to(index_ref[slot, k, 1:2, :], (nvc, LANES)) > 0
        link = []
        for i in range(3):
            for j in range(3):
                row = jnp.where(forward, i * 3 + j, j * 3 + i)
                link.append((glink_ref[slot, k, pl.ds(row, 1), :], sign * glink_ref[slot, k, pl.ds(9 + row, 1), :]))
        for t in range(tiles):
            for part in range(chunks):
                near = []
                for c in range(comps):
                    first = jnp.take_along_axis(own_refs[part][t, ka, c], lanes, axis=1)
                    second = jnp.take_along_axis(own_refs[part][t, kb, c], lanes, axis=1)
                    near.append(jnp.where(take_b, second, first))
                at = pl.ds(place(t, 0, chunks * nvc) + part * nvc, nvc)
                for i in range(3):
                    dr, di = 0.0, 0.0
                    for j in range(3):
                        lr, li = link[i * 3 + j]
                        dr = dr + lr * near[j] - li * near[3 + j]
                        di = di + lr * near[3 + j] + li * near[j]
                    disp[slot, i, at, :] = dr
                    disp[slot, 3 + i, at, :] = di

    for r in range(slots * moms):
        slot, p = divmod(r, moms)
        co = trig_ref[k, p : p + 1, :]
        si = trig_ref[k, moms + p : moms + p + 1, :]
        for i in range(3):
            dr, di = disp[slot, i], disp[slot, 3 + i]
            for part, value in ((0, co * dr + si * di), (1, co * di - si * dr)):
                high, low = split(value)
                first = part * half + i * LANES
                dhi[r * cols : (r + 1) * cols, first : first + LANES] = high
                dlo[r * cols : (r + 1) * cols, first : first + LANES] = low
    acc_ref[...] += jnp.dot(
        jnp.concatenate([dhi[...], dhi[...], dlo[...]], axis=1), whole[...], preferred_element_type=jnp.float32
    )

    @pl.when(k == kt - 1)
    def _():
        span = moms * cols
        for slot in range(slots):
            for part in range(2):
                block = acc_ref[slot * span : (slot + 1) * span, part * rows : (part + 1) * rows]
                first = (slot * 2 + part) * span
                turned[:, first : first + span] = norm * block.T
        part = rows // tiles
        for s in range(tiles):
            out_refs[s][...] = turned[pl.ds(pl.multiple_of(lax.rem(mine + s, tiles) * part, 8), part), :]


def along_tiles(value, steps):
    if steps == 0:
        return value
    count = lax.axis_size("tile")
    return lax.ppermute(value, "tile", [(i, (i + steps) % count) for i in range(count)])


def vec_cores():
    return 2 if lax.axis_size("vec") % 2 == 0 else 1


def over_chips(value):
    count = lax.axis_size("vec")
    blocks = [value]
    for step in range(vec_cores(), count, vec_cores()):
        blocks.append(lax.ppermute(value, "vec", [(i, (i + step) % count) for i in range(count)]))
    return blocks


def over_cores(blocks):
    if vec_cores() == 1:
        return []
    count = lax.axis_size("vec")
    return [lax.ppermute(block, "vec", [(i, i ^ 1) for i in range(count)]) for block in blocks]


def block_owners():
    count, here = lax.axis_size("vec"), lax.axis_index("vec")
    owner = [lax.rem(here - step + count, count) for step in range(0, count, vec_cores())]
    if vec_cores() == 2:
        owner += [other + 1 - 2 * (here % 2) for other in owner]
    return jnp.stack(owner).astype(jnp.int32)


def local(vectors, links, momenta, directions):
    nv = vectors.shape[1]
    sites = vectors.shape[3]
    tiles = lax.axis_size("tile")
    vecs = lax.axis_size("vec")
    tile = lax.axis_index("tile")
    slots = directions.shape[0]
    moms = momenta.shape[0]
    nvt = nv // tiles
    chunks = 2 if nvt % 16 == 0 else 1
    nvc = nvt // chunks
    kt = sites // LANES
    nt = kt * tiles
    extent_x = sites * tiles // PLANE
    norm = 1.0 / math.sqrt(3.0 * sites * tiles)
    f32 = jnp.float32
    smem = pl.BlockSpec(memory_space=pltpu.SMEM)
    vmem = pl.BlockSpec(memory_space=pltpu.VMEM)

    heading = directions % 3
    uses_y = jnp.any(heading == 1)
    uses_x = jnp.any(heading == 0)
    mode = jnp.where(uses_y, jnp.where(uses_x, 2, 0), 1).astype(jnp.int32)
    scal = jnp.concatenate([jnp.stack([mode, tile.astype(jnp.int32)]), directions.astype(jnp.int32)])

    parts = jnp.transpose(vectors, (0, 2, 1, 3)).reshape(6, tiles, chunks, nvc, sites)
    parts = jnp.transpose(parts, (2, 1, 0, 3, 4)).reshape(chunks, tiles, 6 * nvc, sites)
    share = sites // vecs
    link_share = lax.dynamic_slice_in_dim(links.reshape(54, sites), lax.axis_index("vec") * share, share, 1)
    shares = [along_tiles(link_share, s) for s in range(tiles)]
    shares, momenta, directions = lax.optimization_barrier((shares, momenta, directions))
    heading = directions % 3
    gauge = lax.all_gather(jnp.stack(shares), "vec", axis=0)
    fields = []
    for c in range(chunks):
        sent = [lax.dynamic_index_in_dim(parts[c], lax.rem(tile + s, tiles), 0, keepdims=False) for s in range(tiles)]
        if c > 0:
            for s in range(1, tiles):
                fields[c - 1][s], sent[s] = lax.optimization_barrier((fields[c - 1][s], sent[s]))
        fields.append([along_tiles(block, s) for s, block in enumerate(sent)])

    k = jnp.arange(kt, dtype=jnp.int32)[:, None]
    lane = jnp.arange(LANES, dtype=jnp.int32)[None]

    def pick(options):
        return jnp.where(mode == 0, options[0], jnp.where(mode == 1, options[1], options[2]))

    coords = [piece_coords(m, tile, tiles, k, lane) for m in range(3)]
    x, y, z = (pick([jnp.broadcast_to(c[axis], (kt, LANES)) for c in coords]) for axis in range(3))
    start_x = jnp.where(mode == 0, tile * (sites // PLANE), 0)

    def part(axis, coord, extent):
        return jnp.mod(momenta[:, axis, None, None] * coord[None], extent).astype(f32) / extent

    angle = 2.0 * math.pi * (part(0, x + start_x, extent_x) + part(1, y, LY) + part(2, z, LZ))
    trig = jnp.transpose(jnp.concatenate([jnp.cos(angle), jnp.sin(angle)]), (1, 0, 2))

    index, spots = [], []
    for slot in range(slots):
        d = directions[slot]
        step = jnp.where(d < 3, 1, -1)
        xs = jnp.mod(x + jnp.where(heading[slot] == 0, step, 0), extent_x)
        ys = jnp.mod(y + jnp.where(heading[slot] == 1, step, 0), LY)
        zs = jnp.mod(z + jnp.where(heading[slot] == 2, step, 0), LZ)
        found = [piece_index(m, tile, tiles, xs, ys, zs) for m in range(3)]
        ks, ls = (pick([f[i] for f in found]) for i in range(2))
        ka, kb = jnp.min(ks, axis=1), jnp.max(ks, axis=1)
        index.append(jnp.stack([ls, (ks == kb[:, None]).astype(jnp.int32)], axis=1))
        spots.append(jnp.concatenate([ka, kb, (d < 3).astype(jnp.int32)[None]]))
    owner = block_owners()
    spots.append(jnp.broadcast_to(tile.astype(jnp.int32), spots[0].shape))
    spots.append(jnp.pad(owner, (0, 2 * kt + 1 - vecs)))
    index, spots = jnp.stack(index), jnp.stack(spots).astype(jnp.int32)

    fields[0][0], trig, index, spots = lax.optimization_barrier((fields[0][0], trig, index, spots))

    piece_shapes = (jax.ShapeDtypeStruct((kt, 6, nvc, LANES), f32),) * tiles
    link_shape = (6, nt, 18, LANES)
    owns, lefts = [], []
    for c in range(chunks):
        scratch = [pltpu.VMEM((nt, 6, nvc, LANES), f32)] * 2
        call = functools.partial(
            pl.pallas_call,
            functools.partial(filter_kernel, tiles, kt, nvc, c == 0),
            scratch_shapes=scratch,
            compiler_params=pltpu.CompilerParams(vmem_limit_bytes=48 << 20),
            cost_estimate=pl.CostEstimate(
                flops=250 * ITERS * 432 * nvc * nt * LANES, bytes_accessed=48 * nvc * nt * LANES, transcendentals=0
            ),
            name="chebyshev",
        )
        if c == 0:
            *pieces, glink, turned = call(
                out_shape=(
                    *piece_shapes,
                    jax.ShapeDtypeStruct((slots, kt, 18, LANES), f32),
                    jax.ShapeDtypeStruct(link_shape, f32),
                ),
                in_specs=[smem] + [vmem] * (tiles + 1),
                out_specs=(vmem,) * (tiles + 2),
            )(scal, *fields[c], gauge)
        else:
            pieces = call(out_shape=piece_shapes, in_specs=[smem] + [vmem] * (tiles + 1), out_specs=(vmem,) * tiles)(
                scal, *fields[c], turned
            )
        if c + 1 < chunks:
            fields[c + 1], pieces = lax.optimization_barrier((fields[c + 1], pieces))
        if c > 0:
            pieces = list(pieces)
            for s in range(1, tiles):
                own[s], pieces[s] = lax.optimization_barrier((own[s], pieces[s]))
            owns[c - 1] = jnp.stack(own)
        own = [along_tiles(pieces[s], s) for s in range(tiles)]
        owns.append(jnp.stack(own))
    for c in range(chunks):
        if nvc % 8:
            owns[c] = owns[c][jnp.mod(tile - jnp.arange(tiles, dtype=jnp.int32), tiles)]
        lefts.append(over_chips(owns[c]))
        if c == 1:
            lefts[0][1:], owns[1] = lax.optimization_barrier((lefts[0][1:], owns[1]))
            lefts[1][0] = owns[1]

    rows, cols = vecs * tiles * nvc, nv
    depth = 6 * LANES
    bf16 = jnp.bfloat16
    mine = []
    for c in range(chunks):
        near, far = lefts[c][:1], lefts[c][1:]
        twins = over_cores(near)
        if c > 0:
            far, partial_rows = lax.optimization_barrier((far, partial_rows))
        left = near + far + twins + over_cores(far)
        if nvc % 8:
            left = list(jnp.stack(left)[jnp.argsort(owner)])
        if c > 0:
            mine.append(functools.reduce(jnp.add, [along_tiles(partial_rows[s], s) for s in range(tiles)]))
        partial_rows = pl.pallas_call(
            functools.partial(contract_kernel, vecs, chunks, slots, moms, norm),
            grid=(kt,),
            out_shape=(jax.ShapeDtypeStruct((rows // tiles, slots * 2 * moms * cols), f32),) * tiles,
            in_specs=[smem]
            + [pl.BlockSpec((tiles, 1, 6, nvc, LANES), lambda i: (0, i, 0, 0, 0))] * vecs
            + [vmem] * (chunks + 3),
            out_specs=(vmem,) * tiles,
            scratch_shapes=[
                pltpu.VMEM((rows, depth), f32),
                pltpu.VMEM((slots, 6, cols, LANES), f32),
                pltpu.VMEM((3 * depth, 2 * rows), bf16),
                pltpu.VMEM((slots * moms * cols, depth), bf16),
                pltpu.VMEM((slots * moms * cols, depth), bf16),
                pltpu.VMEM((slots * moms * cols, 2 * rows), f32),
                pltpu.VMEM((rows, slots * 2 * moms * cols), f32),
            ],
            compiler_params=pltpu.CompilerParams(vmem_limit_bytes=48 << 20),
            cost_estimate=pl.CostEstimate(
                flops=24 * rows * slots * moms * cols * 6 * sites, bytes_accessed=32 * rows * sites, transcendentals=0
            ),
            name="contract",
        )(spots, *left, *owns, trig, glink, index)
    mine.append(functools.reduce(jnp.add, [along_tiles(partial_rows[s], s) for s in range(tiles)]))
    mine = [m.reshape(-1, nvc, slots * 2 * moms * cols) for m in mine]
    return jnp.stack(mine, axis=1).reshape(nv * vecs // tiles, slots, 2, moms, cols)


def solution(mesh):
    return jax.shard_map(
        local,
        mesh=mesh,
        in_specs=(
            P(None, "vec", None, ("groups", "tile")),
            P(None, None, None, None, ("groups", "tile")),
            P(),
            P(),
        ),
        out_specs=P(("groups", "tile"), None, None, None, "vec"),
        check_vma=False,
    )
```

```python
import functools
import math

import jax
import jax.numpy as jnp
from jax import lax
from jax.experimental import pallas as pl
from jax.experimental.pallas import tpu as pltpu
from jax.sharding import PartitionSpec as P

LY = 16
LZ = 32
ITERS = 4
LANES = 128
PLANE = LY * LZ
QP = PLANE // LANES
YLO = LANES // LZ

hop_scale = 0.125


def piece_coords(mode, tile, tiles, k, lane):
    wy = (LY // tiles) * LZ
    bz = LZ // tiles
    if mode == 0:
        site = k * LANES + lane
        return site // PLANE, site % PLANE // LZ, site % LZ
    if mode == 1:
        flat = k * LANES + lane
        return flat // wy, tile * (LY // tiles) + flat % wy // LZ, lane % LZ
    slot = k * tiles + (lane % LZ) // bz
    return slot // QP, YLO * (slot % QP) + lane // LZ, tile * bz + lane % bz


def piece_index(mode, tile, tiles, x, y, z):
    wy = (LY // tiles) * LZ
    bz = LZ // tiles
    if mode == 0:
        site = x * PLANE + y * LZ + z
        return site // LANES, site % LANES
    if mode == 1:
        flat = x * wy + (y - tile * (LY // tiles)) * LZ + z
        return flat // LANES, flat % LANES
    slot = x * QP + y // YLO
    return slot // tiles, (y % YLO) * LZ + (slot % tiles) * bz + (z - tile * bz)


def pack_piece(mode, tiles, tile, read, write, kt):
    lane = lax.broadcasted_iota(jnp.int32, (1, LANES), 1)
    wy = (LY // tiles) * LZ
    bz = LZ // tiles

    def joined(indices, shifts, owner):
        out = None
        for j, (index, shift) in enumerate(zip(indices, shifts)):
            part = pltpu.roll(read(index), lax.rem(shift + 2 * LANES, LANES), 1)
            out = part if out is None else jnp.where(owner == j, part, out)
        return out

    def one(k, carry):
        if mode == 0:
            value = read(tile * kt + k)
        elif mode == 1 and wy >= LANES:
            per = wy // LANES
            value = read((k // per) * QP + tile * per + k % per)
        elif mode == 1:
            nx = LANES // wy
            first = k * nx * QP + (tile * wy) // LANES
            off = (tile * wy) % LANES
            value = joined([first + j * QP for j in range(nx)], [wy * j - off for j in range(nx)], lane // wy)
        else:
            shifts = [(j - tile) * bz for j in range(tiles)]
            value = joined([k * tiles + j for j in range(tiles)], shifts, (lane % LZ) // bz)
        write(k, value)
        return carry

    lax.fori_loop(0, kt, one, 0, unroll=tiles <= 4)


def filter_kernel(tiles, vecs, kt, rows, with_links, *refs):
    scal, slab_refs, refs = refs[0], refs[1 : 1 + tiles], refs[1 + tiles :]
    if with_links:
        link_refs, piece_refs, refs = refs[:vecs], refs[vecs : vecs + tiles], refs[vecs + tiles :]
        glink_ref, l_ref, a_ref, b_ref = refs
        slots = glink_ref.shape[0]
    else:
        l_ref, piece_refs, (a_ref, b_ref) = refs[0], refs[1 : 1 + tiles], refs[1 + tiles :]
    mine = scal[1]
    comps = 6
    nt = tiles * kt
    lx = nt // QP
    lane = lax.broadcasted_iota(jnp.int32, (1, LANES), 1)
    depth = lane % LZ

    def at(x, q):
        return x * QP + q

    def moved(get, x, q, axis, step):
        n = at(x, q)
        if axis == 0:
            return get(at(lax.rem(x + step + lx, lx), q))
        if axis == 1:
            here, there = get(n), get(at(x, (q + step) % QP))
            if step > 0:
                return rolled(jnp.where(lane < LZ, there, here), LANES - LZ)
            return rolled(jnp.where(lane >= LANES - LZ, there, here), LZ)
        here = get(n)
        if step > 0:
            return jnp.where(depth == LZ - 1, rolled(here, LZ - 1), rolled(here, LANES - 1))
        return jnp.where(depth == 0, rolled(here, LANES - LZ + 1), rolled(here, 1))

    def rolled(value, shift):
        return pltpu.roll(value, shift, value.ndim - 1)

    for s in range(tiles):
        t = lax.rem(mine - s + tiles, tiles)
        for k in range(kt):
            lanes = slice(k * LANES, (k + 1) * LANES)
            for c in range(comps):
                a_ref[t * kt + k, c] = slab_refs[s][c * rows : (c + 1) * rows, lanes]
            if with_links:
                share = kt // vecs
                block, part = divmod(k, share)
                n = t * kt + scal[2 + slots + block] * share + part
                for m in range(3):
                    l_ref[m, n] = link_refs[block][s, 18 * m : 18 * m + 18, part * LANES : (part + 1) * LANES]

    if with_links:

        def shift_links(x, carry):
            for q in range(QP):
                for m in range(3):
                    l_ref[3 + m, at(x, q)] = moved(lambda i: l_ref[m, i], x, q, m, -1)
            return carry

        lax.fori_loop(0, lx, shift_links, 0)

    def hop(src, x, q):
        n = at(x, q)
        acc = [None] * comps
        for m in range(3):
            for side in (0, 1):
                near = [moved(lambda i: src[i, c], x, q, m, 1 - 2 * side) for c in range(comps)]
                for i in range(3):
                    for j in range(3):
                        row = i * 3 + j if side == 0 else j * 3 + i
                        lr = l_ref[3 * side + m, n, row : row + 1, :]
                        li = l_ref[3 * side + m, n, 9 + row : 10 + row, :]
                        fr, fi = near[j], near[3 + j]
                        if side == 0:
                            re = lr * fr - li * fi
                            im = lr * fi + li * fr
                        else:
                            re = lr * fr + li * fi
                            im = lr * fi - li * fr
                        acc[i] = re if acc[i] is None else acc[i] + re
                        acc[3 + i] = im if acc[3 + i] is None else acc[3 + i] + im
        return acc

    src, dst = a_ref, b_ref
    for order in range(ITERS):

        def body(x, carry, src=src, dst=dst, order=order):
            for q in range(QP):
                n = x * QP + q
                acc = hop(src, x, q)
                for c in range(comps):
                    if order == 0:
                        dst[n, c] = hop_scale * acc[c]
                    else:
                        dst[n, c] = (2.0 * hop_scale) * acc[c] - dst[n, c]
            return carry

        lax.fori_loop(0, lx, body, 0)
        src, dst = dst, src

    for mode in range(3):

        @pl.when(scal[0] == mode)
        def _():
            for s in range(tiles):
                for c in range(comps):

                    def write(k, value, s=s, c=c):
                        piece_refs[s][k, c] = value

                    pack_piece(mode, tiles, lax.rem(mine + s, tiles), lambda n, c=c: src[n, c], write, kt)
            if with_links:
                for slot in range(glink_ref.shape[0]):

                    def write(k, value, slot=slot):
                        glink_ref[slot, k] = value

                    pack_piece(mode, tiles, mine, lambda n, slot=slot: l_ref[scal[2 + slot], n], write, kt)


def contract_kernel(vecs, chunks, slots, moms, norm, scal, *refs):
    left_refs, own_refs, refs = refs[:vecs], refs[vecs : vecs + chunks], refs[vecs + chunks :]
    tiles, nvc = own_refs[0].shape[0], own_refs[0].shape[3]
    (trig_ref, glink_ref, index_ref), out_refs, refs = refs[:3], refs[3 : 3 + tiles], refs[3 + tiles :]
    side, disp, whole, dhi, dlo, acc_ref, turned = refs
    k = pl.program_id(0)
    rows = vecs * tiles * nvc
    cols = tiles * nvc * chunks
    comps = 6
    kt = pl.num_programs(0)
    depth = comps * LANES
    half = 3 * LANES

    mine = scal[slots, 0]

    def split(value):
        high = value.astype(jnp.bfloat16)
        return high, (value - high.astype(jnp.float32)).astype(jnp.bfloat16)

    def place(s, outer, count):
        if nvc % 8:
            return (outer * tiles + s) * count
        return pl.multiple_of((outer * tiles + lax.rem(mine - s + tiles, tiles)) * count, 8)

    @pl.when(k == 0)
    def _():
        acc_ref[...] = jnp.zeros_like(acc_ref)

    for v in range(vecs):
        for t in range(tiles):
            at = pl.ds(place(t, v if nvc % 8 else scal[slots + 1, v], nvc), nvc)
            for c in range(comps):
                side[at, c * LANES : (c + 1) * LANES] = left_refs[v][t, 0, c]
    for c in range(3):
        rh, rl = split(side[:, c * LANES : (c + 1) * LANES].T)
        ih, il = split(side[:, half + c * LANES : half + (c + 1) * LANES].T)
        for third, re, im in ((0, rh, ih), (1, rl, il), (2, rh, ih)):
            first = third * depth + c * LANES
            whole[first : first + LANES, 0:rows] = re
            whole[first + half : first + half + LANES, 0:rows] = im
            whole[first : first + LANES, rows : 2 * rows] = -im
            whole[first + half : first + half + LANES, rows : 2 * rows] = re

    for slot in range(slots):
        ka, kb = scal[slot, k], scal[slot, kt + k]
        forward = scal[slot, 2 * kt] > 0
        sign = jnp.where(forward, 1.0, -1.0)
        lanes = jnp.broadcast_to(index_ref[slot, k, 0:1, :], (nvc, LANES))
        take_b = jnp.broadcast_to(index_ref[slot, k, 1:2, :], (nvc, LANES)) > 0
        link = []
        for i in range(3):
            for j in range(3):
                row = jnp.where(forward, i * 3 + j, j * 3 + i)
                link.append((glink_ref[slot, k, pl.ds(row, 1), :], sign * glink_ref[slot, k, pl.ds(9 + row, 1), :]))
        for t in range(tiles):
            for part in range(chunks):
                near = []
                for c in range(comps):
                    first = jnp.take_along_axis(own_refs[part][t, ka, c], lanes, axis=1)
                    second = jnp.take_along_axis(own_refs[part][t, kb, c], lanes, axis=1)
                    near.append(jnp.where(take_b, second, first))
                at = pl.ds(place(t, 0, chunks * nvc) + part * nvc, nvc)
                for i in range(3):
                    dr, di = 0.0, 0.0
                    for j in range(3):
                        lr, li = link[i * 3 + j]
                        dr = dr + lr * near[j] - li * near[3 + j]
                        di = di + lr * near[3 + j] + li * near[j]
                    disp[slot, i, at, :] = dr
                    disp[slot, 3 + i, at, :] = di

    for r in range(slots * moms):
        slot, p = divmod(r, moms)
        co = trig_ref[k, p : p + 1, :]
        si = trig_ref[k, moms + p : moms + p + 1, :]
        for i in range(3):
            dr, di = disp[slot, i], disp[slot, 3 + i]
            for part, value in ((0, co * dr + si * di), (1, co * di - si * dr)):
                high, low = split(value)
                first = part * half + i * LANES
                dhi[r * cols : (r + 1) * cols, first : first + LANES] = high
                dlo[r * cols : (r + 1) * cols, first : first + LANES] = low
    acc_ref[...] += jnp.dot(
        jnp.concatenate([dhi[...], dhi[...], dlo[...]], axis=1), whole[...], preferred_element_type=jnp.float32
    )

    @pl.when(k == kt - 1)
    def _():
        span = moms * cols
        for slot in range(slots):
            for part in range(2):
                block = acc_ref[slot * span : (slot + 1) * span, part * rows : (part + 1) * rows]
                first = (slot * 2 + part) * span
                turned[:, first : first + span] = norm * block.T
        part = rows // tiles
        for s in range(tiles):
            out_refs[s][...] = turned[pl.ds(pl.multiple_of(lax.rem(mine + s, tiles) * part, 8), part), :]


def along_tiles(value, steps):
    if steps == 0:
        return value
    count = lax.axis_size("tile")
    return lax.ppermute(value, "tile", [(i, (i + steps) % count) for i in range(count)])


def vec_cores():
    return 2 if lax.axis_size("vec") % 2 == 0 else 1


def over_chips(value):
    count = lax.axis_size("vec")
    blocks = [value]
    for step in range(vec_cores(), count, vec_cores()):
        blocks.append(lax.ppermute(value, "vec", [(i, (i + step) % count) for i in range(count)]))
    return blocks


def over_cores(blocks):
    if vec_cores() == 1:
        return []
    count = lax.axis_size("vec")
    return [lax.ppermute(block, "vec", [(i, i ^ 1) for i in range(count)]) for block in blocks]


def block_owners():
    count, here = lax.axis_size("vec"), lax.axis_index("vec")
    owner = [lax.rem(here - step + count, count) for step in range(0, count, vec_cores())]
    if vec_cores() == 2:
        owner += [other + 1 - 2 * (here % 2) for other in owner]
    return jnp.stack(owner).astype(jnp.int32)


def local(vectors, links, momenta, directions):
    nv = vectors.shape[1]
    sites = vectors.shape[3]
    tiles = lax.axis_size("tile")
    vecs = lax.axis_size("vec")
    tile = lax.axis_index("tile")
    slots = directions.shape[0]
    moms = momenta.shape[0]
    nvt = nv // tiles
    chunks = 2 if nvt % 16 == 0 else 1
    nvc = nvt // chunks
    kt = sites // LANES
    nt = kt * tiles
    extent_x = sites * tiles // PLANE
    norm = 1.0 / math.sqrt(3.0 * sites * tiles)
    f32 = jnp.float32
    smem = pl.BlockSpec(memory_space=pltpu.SMEM)
    vmem = pl.BlockSpec(memory_space=pltpu.VMEM)

    heading = directions % 3
    uses_y = jnp.any(heading == 1)
    uses_x = jnp.any(heading == 0)
    mode = jnp.where(uses_y, jnp.where(uses_x, 2, 0), 1).astype(jnp.int32)
    scal = jnp.concatenate([jnp.stack([mode, tile.astype(jnp.int32)]), directions.astype(jnp.int32), block_owners()])

    parts = jnp.transpose(vectors, (0, 2, 1, 3)).reshape(6, tiles, chunks, nvc, sites)
    parts = jnp.transpose(parts, (2, 1, 0, 3, 4)).reshape(chunks, tiles, 6 * nvc, sites)
    share = sites // vecs
    link_share = lax.dynamic_slice_in_dim(links.reshape(54, sites), lax.axis_index("vec") * share, share, 1)
    shares = [along_tiles(link_share, s) for s in range(tiles)]
    shares, momenta, directions = lax.optimization_barrier((shares, momenta, directions))
    heading = directions % 3
    gauge = over_chips(jnp.stack(shares))
    gauge = gauge + over_cores(gauge)
    fields = []
    for c in range(chunks):
        sent = [lax.dynamic_index_in_dim(parts[c], lax.rem(tile + s, tiles), 0, keepdims=False) for s in range(tiles)]
        if c > 0:
            for s in range(1, tiles):
                fields[c - 1][s], sent[s] = lax.optimization_barrier((fields[c - 1][s], sent[s]))
        fields.append([along_tiles(block, s) for s, block in enumerate(sent)])

    k = jnp.arange(kt, dtype=jnp.int32)[:, None]
    lane = jnp.arange(LANES, dtype=jnp.int32)[None]

    def pick(options):
        return jnp.where(mode == 0, options[0], jnp.where(mode == 1, options[1], options[2]))

    coords = [piece_coords(m, tile, tiles, k, lane) for m in range(3)]
    x, y, z = (pick([jnp.broadcast_to(c[axis], (kt, LANES)) for c in coords]) for axis in range(3))
    start_x = jnp.where(mode == 0, tile * (sites // PLANE), 0)

    def part(axis, coord, extent):
        return jnp.mod(momenta[:, axis, None, None] * coord[None], extent).astype(f32) / extent

    angle = 2.0 * math.pi * (part(0, x + start_x, extent_x) + part(1, y, LY) + part(2, z, LZ))
    trig = jnp.transpose(jnp.concatenate([jnp.cos(angle), jnp.sin(angle)]), (1, 0, 2))

    index, spots = [], []
    for slot in range(slots):
        d = directions[slot]
        step = jnp.where(d < 3, 1, -1)
        xs = jnp.mod(x + jnp.where(heading[slot] == 0, step, 0), extent_x)
        ys = jnp.mod(y + jnp.where(heading[slot] == 1, step, 0), LY)
        zs = jnp.mod(z + jnp.where(heading[slot] == 2, step, 0), LZ)
        found = [piece_index(m, tile, tiles, xs, ys, zs) for m in range(3)]
        ks, ls = (pick([f[i] for f in found]) for i in range(2))
        ka, kb = jnp.min(ks, axis=1), jnp.max(ks, axis=1)
        index.append(jnp.stack([ls, (ks == kb[:, None]).astype(jnp.int32)], axis=1))
        spots.append(jnp.concatenate([ka, kb, (d < 3).astype(jnp.int32)[None]]))
    owner = block_owners()
    spots.append(jnp.broadcast_to(tile.astype(jnp.int32), spots[0].shape))
    spots.append(jnp.pad(owner, (0, 2 * kt + 1 - vecs)))
    index, spots = jnp.stack(index), jnp.stack(spots).astype(jnp.int32)

    fields[0][0], trig, index, spots = lax.optimization_barrier((fields[0][0], trig, index, spots))

    piece_shapes = (jax.ShapeDtypeStruct((kt, 6, nvc, LANES), f32),) * tiles
    link_shape = (6, nt, 18, LANES)
    owns, lefts = [], []
    for c in range(chunks):
        scratch = [pltpu.VMEM((nt, 6, nvc, LANES), f32)] * 2
        call = functools.partial(
            pl.pallas_call,
            functools.partial(filter_kernel, tiles, vecs, kt, nvc, c == 0),
            scratch_shapes=scratch,
            compiler_params=pltpu.CompilerParams(vmem_limit_bytes=48 << 20),
            cost_estimate=pl.CostEstimate(
                flops=250 * ITERS * 432 * nvc * nt * LANES, bytes_accessed=48 * nvc * nt * LANES, transcendentals=0
            ),
            name="chebyshev",
        )
        if c == 0:
            *pieces, glink, turned = call(
                out_shape=(
                    *piece_shapes,
                    jax.ShapeDtypeStruct((slots, kt, 18, LANES), f32),
                    jax.ShapeDtypeStruct(link_shape, f32),
                ),
                in_specs=[smem] + [vmem] * (tiles + vecs),
                out_specs=(vmem,) * (tiles + 2),
            )(scal, *fields[c], *gauge)
        else:
            pieces = call(out_shape=piece_shapes, in_specs=[smem] + [vmem] * (tiles + 1), out_specs=(vmem,) * tiles)(
                scal, *fields[c], turned
            )
        if c + 1 < chunks:
            fields[c + 1], pieces = lax.optimization_barrier((fields[c + 1], pieces))
        if c > 0:
            pieces = list(pieces)
            for s in range(1, tiles):
                own[s], pieces[s] = lax.optimization_barrier((own[s], pieces[s]))
            owns[c - 1] = jnp.stack(own)
        own = [along_tiles(pieces[s], s) for s in range(tiles)]
        owns.append(jnp.stack(own))
    for c in range(chunks):
        if nvc % 8:
            owns[c] = owns[c][jnp.mod(tile - jnp.arange(tiles, dtype=jnp.int32), tiles)]
        lefts.append(over_chips(owns[c]))
        if c == 1:
            lefts[0][1:], owns[1] = lax.optimization_barrier((lefts[0][1:], owns[1]))
            lefts[1][0] = owns[1]

    rows, cols = vecs * tiles * nvc, nv
    depth = 6 * LANES
    bf16 = jnp.bfloat16
    mine = []
    for c in range(chunks):
        near, far = lefts[c][:1], lefts[c][1:]
        twins = over_cores(near)
        if c > 0:
            far, partial_rows = lax.optimization_barrier((far, partial_rows))
        left = near + far + twins + over_cores(far)
        if nvc % 8:
            left = list(jnp.stack(left)[jnp.argsort(owner)])
        if c > 0:
            mine.append(functools.reduce(jnp.add, [along_tiles(partial_rows[s], s) for s in range(tiles)]))
        partial_rows = pl.pallas_call(
            functools.partial(contract_kernel, vecs, chunks, slots, moms, norm),
            grid=(kt,),
            out_shape=(jax.ShapeDtypeStruct((rows // tiles, slots * 2 * moms * cols), f32),) * tiles,
            in_specs=[smem]
            + [pl.BlockSpec((tiles, 1, 6, nvc, LANES), lambda i: (0, i, 0, 0, 0))] * vecs
            + [vmem] * (chunks + 3),
            out_specs=(vmem,) * tiles,
            scratch_shapes=[
                pltpu.VMEM((rows, depth), f32),
                pltpu.VMEM((slots, 6, cols, LANES), f32),
                pltpu.VMEM((3 * depth, 2 * rows), bf16),
                pltpu.VMEM((slots * moms * cols, depth), bf16),
                pltpu.VMEM((slots * moms * cols, depth), bf16),
                pltpu.VMEM((slots * moms * cols, 2 * rows), f32),
                pltpu.VMEM((rows, slots * 2 * moms * cols), f32),
            ],
            compiler_params=pltpu.CompilerParams(vmem_limit_bytes=48 << 20),
            cost_estimate=pl.CostEstimate(
                flops=24 * rows * slots * moms * cols * 6 * sites, bytes_accessed=32 * rows * sites, transcendentals=0
            ),
            name="contract",
        )(spots, *left, *owns, trig, glink, index)
    mine.append(functools.reduce(jnp.add, [along_tiles(partial_rows[s], s) for s in range(tiles)]))
    mine = [m.reshape(-1, nvc, slots * 2 * moms * cols) for m in mine]
    return jnp.stack(mine, axis=1).reshape(nv * vecs // tiles, slots, 2, moms, cols)


def solution(mesh):
    return jax.shard_map(
        local,
        mesh=mesh,
        in_specs=(
            P(None, "vec", None, ("groups", "tile")),
            P(None, None, None, None, ("groups", "tile")),
            P(),
            P(),
        ),
        out_specs=P(("groups", "tile"), None, None, None, "vec"),
        check_vma=False,
    )
```
